256 devices in a mesh: arc: 16 (over x, y), ord: 16 (over z, core).
Axes of the slice: x: 4, y: 4, z: 8, core: 2. Of those that a mesh axis runs over, the one named last changes fastest.
Arguments:
- obs_colat: float32 [393216], P('arc'), may hold values from 0.12 to 3.0216
- obs_lon: float32 [393216], P('arc'), may hold values from -3.140625 to 3.140625
- obs_value: bfloat16 [393216], P('arc'), may hold values from -6 to 6
- obs_arc: int32 [393216], P('arc'), may hold values from 0 to 16, as said below
- reg_weight: float32 [32, 252], P('ord'), may hold values from 0.1 to 1
Outputs:
- solution: float32 [32, 252], P('ord')
- arc_bias: float32 [256], P('arc')
- residual: float32 [393216], P(('arc', 'ord'))
The draws below stay inside these ranges and needn't reach their ends.
Inputs may be any that keep to these rules, and one draw needn't show every extreme that they name: `obs_arc`: within each arc device's 24576 slots the values never fall, each of 0 to 15 names at least one slot, and the value 16 marks unused slots, which come last. Every arc device uses at least 6144 slots, and some arc device uses all 24576.
All inputs are finite; a program needn't handle non-finite values.
Results may differ from the reference program's by a relative error of at most 0.0055.
Values sent between devices are 32-bit elements; how exact they have to be, the bound alone decides.
A program may use at most 320 MiB of HBM per device.

```python
import math
import jax
import jax.numpy as jnp
import numpy as np
from jax import lax

DEG = 250
BLOCK = 252
ARC_DEV = 16
OBS_DEV = 24576
OBS_TOTAL = 393216
PAIRS = 32
N_ARC = 16


def draw_obs_arc(key, part):
    key = jax.random.fold_in(key, 11)
    key_count, key_full, key_cut = jax.random.split(key, 3)
    devices = OBS_TOTAL // OBS_DEV
    filled = jax.random.randint(key_count, (devices,), OBS_DEV // 4, OBS_DEV + 1).astype(jnp.int32)
    chosen = jax.random.randint(key_full, (), 0, devices).astype(jnp.int32)
    filled = jnp.where(jnp.arange(devices, dtype=jnp.int32) == chosen, OBS_DEV, filled)
    positions = jnp.arange(1, OBS_DEV, dtype=jnp.int32)
    scores = jax.random.randint(key_cut, (devices, OBS_DEV - 1), 0, 65536).astype(jnp.int32) * OBS_DEV + positions[None, :]
    scores = jnp.where(positions[None, :] < filled[:, None], scores, 2 ** 30)
    _, picked = lax.top_k(-scores, ARC_DEV - 1)
    boundaries = picked.astype(jnp.int32) + 1
    slot_ids = jnp.arange(OBS_DEV, dtype=jnp.int32)
    arc_number = jnp.sum((boundaries[:, :, None] <= slot_ids[None, None, :]).astype(jnp.int32), axis=1)
    arc_number = jnp.where(slot_ids[None, :] < filled[:, None], arc_number, ARC_DEV)
    return arc_number.reshape(-1).astype(jnp.int32)


def draw_obs_colat(key, part):
    key = jax.random.fold_in(key, 23)
    key_phase, key_jitter = jax.random.split(key)
    devices = OBS_TOTAL // OBS_DEV
    starting = jax.random.uniform(key_phase, (devices, 1), jnp.float32, 0.0, 2.0 * math.pi)
    along_track = jnp.arange(OBS_DEV, dtype=jnp.float32)[None, :] * (2.0 * math.pi / 1080.0)
    jitter = jax.random.uniform(key_jitter, (devices, OBS_DEV), jnp.float32, -0.01, 0.01)
    amplitude = 0.5 * math.pi - 0.13
    colatitude = 0.5 * math.pi + amplitude * jnp.sin(starting + along_track) + jitter
    return colatitude.reshape(-1).astype(jnp.float32)


def block_scale(rng, shape, shards, smallest, top_value):
    gain = 1.0
    for position, blocks in shards:
        steps = jax.random.uniform(jax.random.fold_in(jax.random.fold_in(rng, 6), position), (blocks,), jnp.float32, smallest / len(shards), top_value / len(shards))
        gain = gain * jnp.repeat(jnp.exp(steps), shape[position] // blocks).reshape((-1,) + (1,) * (len(shape) - 1 - position))
    return gain


def gaussian(stream_key, extent, scale, most, pieces=(), held_as=jnp.bfloat16):
    values = jax.random.normal(stream_key, extent, jnp.float32) * scale
    if len(pieces) > 0:
        values = block_scale(stream_key, extent, pieces, -0.22, 0.18) * values
    return jnp.clip(values, min=-most, max=most).astype(held_as)


def setup_inputs(seed: int = 0) -> dict:
    keys = jax.random.split(jax.random.key(seed), 6)
    obs_colat = draw_obs_colat(jax.random.fold_in(keys[5], 71), 0)
    obs_lon = jnp.clip(jax.random.uniform(keys[1], (OBS_TOTAL,), jnp.float32, -3.140625, 3.140625), -3.140625, 3.140625)
    obs_value = gaussian(keys[2], (OBS_TOTAL,), 1.0, 6.0, ((0, 16),))
    obs_arc = draw_obs_arc(jax.random.fold_in(keys[5], 71), 0)
    reg_weight = jnp.clip(jnp.exp(math.log(1.0) - 2.3025851 * jax.random.uniform(keys[4], (PAIRS, BLOCK), jnp.float32) ** block_scale(keys[4], (PAIRS, BLOCK), ((0, 16),), -0.2, 0.2)), 0.1, 1.0)
    return dict(obs_colat=obs_colat, obs_lon=obs_lon, obs_value=obs_value, obs_arc=obs_arc, reg_weight=reg_weight)


def log_sectoral():
    increments = [0.0, 0.5 * math.log(3.0)] + [0.5 * math.log((2.0 * degree_now + 1.0) / (2.0 * degree_now)) for degree_now in range(2, DEG + 1)]
    return jnp.asarray(np.cumsum(np.array(increments[:DEG + 1])), dtype=jnp.float32)

def design_columns(colatitude, longitude, arc_ids, first_order):
    pair_count = first_order.shape[0]
    observed = (arc_ids < ARC_DEV).astype(jnp.float32)
    orders = jnp.concatenate([first_order, DEG - first_order]).astype(jnp.int32)
    offsets = jnp.concatenate([first_order, jnp.full((pair_count,), -1, jnp.int32)]).astype(jnp.int32)
    order_float = orders.astype(jnp.float32)
    log_table = log_sectoral()
    log_coeff = lax.optimization_barrier(jnp.sum(jnp.where(jnp.arange(DEG + 1, dtype=jnp.int32)[None, :] == orders[:, None], log_table[None, :], 0.0), axis=1))
    cosine = jnp.cos(colatitude)
    sine_theta = jnp.sin(colatitude)
    sectoral = jnp.exp(order_float[:, None] * jnp.log(sine_theta)[None, :] + log_coeff[:, None])
    phases = jnp.cos(order_float[:, None] * longitude[None, :]) * observed[None, :]

    def recurse(carried, column):
        previous, before = carried
        degree = column + offsets
        degree_float = degree.astype(jnp.float32)
        beyond_order = degree > orders
        denominator = jnp.maximum((degree_float - order_float) * (degree_float + order_float), 1.0)
        rising = jnp.where(beyond_order, jnp.sqrt(jnp.maximum((2.0 * degree_float - 1.0) * (2.0 * degree_float + 1.0), 0.0) / denominator), 0.0)
        falling_top = jnp.maximum((2.0 * degree_float + 1.0) * (degree_float + order_float - 1.0) * (degree_float - order_float - 1.0), 0.0)
        falling = jnp.where(beyond_order, jnp.sqrt(falling_top / (denominator * jnp.maximum(2.0 * degree_float - 3.0, 1.0))), 0.0)
        current = rising[:, None] * cosine[None, :] * previous - falling[:, None] * before
        current = jnp.where((degree == orders)[:, None], sectoral, current)
        emitted = jnp.where((degree <= DEG)[:, None], current, 0.0) * phases
        return ((current, previous), (emitted[:pair_count] + emitted[pair_count:]).astype(jnp.bfloat16))
    initial = jnp.zeros((2 * pair_count, colatitude.shape[0]), jnp.float32)
    _, columns = lax.scan(recurse, (initial, initial), jnp.arange(DEG + 2, dtype=jnp.int32), unroll=12)
    return columns

def local_normals(columns, values, arc_ids):
    arc_member = (jnp.arange(ARC_DEV, dtype=jnp.int32)[:, None] == arc_ids[None, :]).astype(jnp.float32)
    counts = lax.optimization_barrier(jnp.sum(arc_member, axis=1))
    weighted = jnp.where(arc_ids < ARC_DEV, values, jnp.zeros_like(values)).astype(jnp.float32)
    wide_columns = columns.astype(jnp.float32)
    normal_part = lax.dot_general(wide_columns, wide_columns, (((2,), (2,)), ((1,), (1,))))
    arc_sums = jnp.einsum('cpr,kr->pkc', wide_columns, arc_member)
    projected = jnp.einsum('cpr,r->pc', wide_columns, weighted)
    arc_target = jnp.einsum('kr,r->k', arc_member, weighted)
    scaled = arc_sums / counts[None, :, None]
    normal_part = normal_part - jnp.einsum('pkc,pkd->pcd', scaled, arc_sums, precision=lax.Precision.HIGHEST)
    right_part = projected - jnp.einsum('pkc,k->pc', arc_sums, arc_target / counts, precision=lax.Precision.HIGHEST)
    return (normal_part, right_part, arc_sums, arc_target, counts)

def solve_pairs(normal_sum, right_sum, regular, first_order, total_rows):
    block_width = normal_sum.shape[-1]
    column_ids = jnp.arange(block_width, dtype=jnp.int32)
    low_order = column_ids[None, :] < (DEG + 1 - first_order)[:, None]
    same_order = (low_order[:, :, None] == low_order[:, None, :]).astype(jnp.float32)
    matrix = same_order * normal_sum / total_rows + jnp.eye(block_width, dtype=jnp.float32)[None, :, :] * regular[:, None, :]
    factor = jnp.linalg.cholesky(matrix)
    target = (right_sum / math.sqrt(total_rows))[:, :, None]
    middle = lax.linalg.triangular_solve(factor, target, left_side=True, lower=True)
    solution = lax.linalg.triangular_solve(factor, middle, left_side=True, lower=True, transpose_a=True)
    return solution[:, :, 0]

def reference(obs_colat, obs_lon, obs_value, obs_arc, reg_weight):
    first_order = jnp.arange(PAIRS, dtype=jnp.int32)
    root_total = math.sqrt(OBS_TOTAL)
    blocks = (obs_colat.reshape(N_ARC, OBS_DEV), obs_lon.reshape(N_ARC, OBS_DEV), obs_value.reshape(N_ARC, OBS_DEV), obs_arc.reshape(N_ARC, OBS_DEV))

    def assemble(carried, block):
        columns = design_columns(block[0], block[1], block[3], first_order)
        normal_part, right_part, arc_sums, arc_target, counts = local_normals(columns, block[2], block[3])
        return ((carried[0] + normal_part, carried[1] + right_part), (arc_sums, arc_target, counts))
    start_zero = (jnp.zeros((PAIRS, BLOCK, BLOCK), jnp.float32), jnp.zeros((PAIRS, BLOCK), jnp.float32))
    (normal_sum, right_sum), (arc_sums, arc_target, counts) = lax.scan(assemble, start_zero, blocks)
    solution = solve_pairs(normal_sum, right_sum, reg_weight, first_order, OBS_TOTAL)

    def fitting(block):
        columns = design_columns(block[0], block[1], block[3], first_order)
        return jnp.einsum('cpr,pc->r', columns.astype(jnp.float32), solution, precision=lax.Precision.HIGHEST) / root_total
    fitted = lax.map(fitting, blocks)
    offsets = jnp.einsum('apkc,pc->ak', arc_sums, solution, precision=lax.Precision.HIGHEST) / root_total
    arc_bias = (arc_target - offsets) / counts
    arc_member = (jnp.arange(ARC_DEV, dtype=jnp.int32)[None, :, None] == blocks[3][:, None, :]).astype(jnp.float32)
    bias_rows = lax.optimization_barrier(jnp.sum(arc_member * arc_bias[:, :, None], axis=1))
    residual = jnp.where(blocks[3] < ARC_DEV, blocks[2].astype(jnp.float32) - fitted - bias_rows, 0.0)
    return (solution, arc_bias.reshape(-1), residual.reshape(-1))
```

```python
import functools
import math

import jax
import jax.numpy as jnp
import numpy as np
from jax import lax
from jax.experimental import pallas as pl
from jax.experimental.pallas import tpu as pltpu
from jax.sharding import PartitionSpec as P

DEG = 250
BLOCK = 252
ARC_DEV = 16
WIDE = 256
ROWS = WIDE + ARC_DEV
VALUE_ROW = 255
CHUNK = 4096
TILES = CHUNK // 128
GROUPS = CHUNK // 1024
PANEL = 64
MESH = pl.DeviceIdType.MESH
MIB = 1024 * 1024
HIGHEST = lax.Precision.HIGHEST


def log_sectoral():
    increments = [0.0, 0.5 * math.log(3.0)] + [
        0.5 * math.log((2.0 * degree_now + 1.0) / (2.0 * degree_now))
        for degree_now in range(2, DEG + 1)
    ]
    return np.cumsum(np.array(increments[: DEG + 1])).astype(np.float32)


def recursion_table(pairs):
    table = np.zeros((pairs, 2, WIDE), np.float64)
    for pair in range(pairs):
        for column in range(BLOCK):
            low = column < DEG + 1 - pair
            order = pair if low else DEG - pair
            degree = pair + column if low else column - 1
            if degree == order:
                table[pair, 0, column] = 0.0
                table[pair, 1, column] = -1.0
                continue
            denominator = float((degree - order) * (degree + order))
            table[pair, 0, column] = math.sqrt(
                (2.0 * degree - 1.0) * (2.0 * degree + 1.0) / denominator
            )
            table[pair, 1, column] = math.sqrt(
                max((2.0 * degree + 1.0) * (degree + order - 1.0) * (degree - order - 1.0), 0.0)
                / (denominator * max(2.0 * degree - 3.0, 1.0))
            )
    return table.astype(np.float32)


def design_kernel(
    coef_ref,
    t_ref,
    seed_ref,
    value_ref,
    member_ref,
    counts_ref,
    design_ref,
    normal_ref,
    sums_ref,
    flat,
    total,
):
    step = pl.program_id(0)
    first_pair = lax.axis_index("ord") * 2
    starts = [DEG + 1 - first_pair, DEG - first_pair]
    chains = [(p, v) for p in range(2) for v in range(GROUPS)]

    @pl.when(step == 0)
    def _():
        total[...] = jnp.zeros_like(total)
        for tile in range(2 * TILES):
            flat[tile * WIDE + BLOCK - 4 : tile * WIDE + WIDE, :] = jnp.zeros(
                (WIDE - BLOCK + 4, 128), jnp.float32
            )

    t = [t_ref[v * 8 : v * 8 + 8, :] for v in range(GROUPS)]
    seed_low = tuple(seed_ref[p, v * 8 : v * 8 + 8, :] for p, v in chains)

    def place(p, v, column, data):
        flat[pl.ds((p * TILES + v * 8) * WIDE + column, 8, stride=WIDE), :] = data

    for p in range(2):
        for v in range(GROUPS):
            place(p, v, VALUE_ROW, value_ref[v * 8 : v * 8 + 8, :])

    def columns4(block, previous, before, seeds):
        for inner in range(4):
            column = block * 4 + inner
            rising = [coef_ref[p * 2 * WIDE + column] for p in range(2)]
            falling = [coef_ref[p * 2 * WIDE + WIDE + column] for p in range(2)]
            current = []
            for i, (p, v) in enumerate(chains):
                older = before[i]
                if seeds is not None:
                    older = jnp.where(column == starts[p], seeds[i], older)
                now = rising[p] * (t[v] * previous[i]) - falling[p] * older
                place(p, v, column, now)
                current.append(now)
            before, previous = previous, tuple(current)
        return previous, before

    zeros = tuple(jnp.zeros((8, 128), jnp.float32) for _ in chains)
    turn = starts[0] // 4
    carried = lax.fori_loop(
        0, turn, lambda block, c: columns4(block, c[0], c[1], None), (zeros, seed_low)
    )
    seed_high = tuple(seed_ref[2 + p, v * 8 : v * 8 + 8, :] for p, v in chains)
    carried = columns4(turn, carried[0], carried[1], seed_high)
    lax.fori_loop(
        turn + 1, BLOCK // 4, lambda block, c: columns4(block, c[0], c[1], None), carried
    )

    for p in range(2):
        design_ref[p, WIDE:ROWS, :] = member_ref[...]

        def convert(tile, _, p=p):
            lane = pl.multiple_of(tile * 128, 128)
            source = pl.multiple_of((p * TILES + tile) * WIDE, WIDE)
            design_ref[p, 0:WIDE, pl.ds(lane, 128)] = flat[pl.ds(source, WIDE), :].astype(
                jnp.bfloat16
            )
            return 0

        lax.fori_loop(0, TILES, convert, 0)

        def product(part, _, p=p):
            lane = pl.multiple_of(part * 1024, 1024)
            total[p] += lax.dot_general(
                design_ref[p, :, pl.ds(lane, 1024)],
                design_ref[p, 0:WIDE, pl.ds(lane, 1024)],
                (((1,), (1,)), ((), ())),
                preferred_element_type=jnp.float32,
            )
            return 0

        lax.fori_loop(0, CHUNK // 1024, product, 0)

    @pl.when(step == pl.num_programs(0) - 1)
    def _():
        for p in range(2):
            sums = total[p, WIDE:ROWS, :]
            counts = jnp.concatenate([counts_ref[...], counts_ref[...]], axis=1)
            scaled = sums / counts
            normal_ref[p] = total[p, 0:WIDE, :] - lax.dot_general(
                scaled,
                sums,
                (((0,), (0,)), ((), ())),
                precision=HIGHEST,
                preferred_element_type=jnp.float32,
            )
            sums_ref[p] = sums


def reduce_kernel(n, part_ref, out_ref, landed, send1, recv1, send2, recv2):
    me = lax.axis_index("arc")
    barrier = pltpu.get_barrier_semaphore()

    def greet(k, _):
        pl.semaphore_signal(
            barrier, inc=1, device_id={"arc": lax.rem(me + k, n)}, device_id_type=MESH
        )
        return 0

    lax.fori_loop(1, n, greet, 0)
    pl.semaphore_wait(barrier, n - 1)

    def scatter(k):
        peer = lax.rem(me + k, n)
        return pltpu.make_async_remote_copy(
            src_ref=part_ref.at[peer],
            dst_ref=landed.at[k],
            send_sem=send1.at[k],
            recv_sem=recv1.at[k],
            device_id={"arc": peer},
            device_id_type=MESH,
        )

    def gather(k):
        peer = lax.rem(me + k, n)
        return pltpu.make_async_remote_copy(
            src_ref=out_ref.at[me],
            dst_ref=out_ref.at[me],
            send_sem=send2.at[k],
            recv_sem=recv2.at[k],
            device_id={"arc": peer},
            device_id_type=MESH,
        )

    def start(make):
        def body(k, _):
            make(k).start()
            return 0

        lax.fori_loop(1, n, body, 0)

    def finish(make):
        def body(k, _):
            make(k).wait_send()
            return 0

        lax.fori_loop(1, n, body, 0)

    start(scatter)
    out_ref[me] = part_ref[me]

    def add(k, _):
        scatter(k).wait_recv()
        out_ref[me] = out_ref[me] + landed[k]
        return 0

    lax.fori_loop(1, n, add, 0)
    start(gather)

    def arrive(k, _):
        source = lax.rem(me - k + n, n)
        pltpu.make_async_remote_copy(
            src_ref=out_ref.at[source],
            dst_ref=out_ref.at[source],
            send_sem=send2.at[k],
            recv_sem=recv2.at[k],
            device_id={"arc": source},
            device_id_type=MESH,
        ).wait_recv()
        return 0

    lax.fori_loop(1, n, arrive, 0)
    finish(scatter)
    finish(gather)


def solve_kernel(
    total_rows,
    normal_ref,
    regular_ref,
    sums_ref,
    design_hbm,
    solution_ref,
    share_ref,
    design,
    work,
    copied,
    *,
    parts,
):
    first_pair = lax.axis_index("ord") * 2
    rows_here = design_hbm.shape[2]
    width = rows_here // parts
    copies = []
    for part in range(parts):
        span = pl.ds(part * width, width)
        copy = pltpu.make_async_copy(
            design_hbm.at[:, pl.ds(0, WIDE), span], design.at[:, :, span], copied.at[part]
        )
        copy.start()
        copies.append(copy)

    row_ids = lax.broadcasted_iota(jnp.int32, (WIDE, WIDE), 0)
    column_ids = lax.broadcasted_iota(jnp.int32, (WIDE, WIDE), 1)
    eye = row_ids == column_ids
    for p in range(2):
        border = DEG + 1 - first_pair - p
        real = (row_ids < BLOCK) & (column_ids < BLOCK)
        same = ((row_ids < border) == (column_ids < border)) & real
        normal = normal_ref[p]
        matrix = jnp.where(same, normal / total_rows, 0.0)
        matrix = matrix + jnp.where(eye, regular_ref[p], 0.0)
        right = jnp.where(row_ids < BLOCK, normal / math.sqrt(total_rows), 0.0)
        work[p] = jnp.where(column_ids == VALUE_ROW, right, matrix)

    for panel in range(WIDE // PANEL):
        top = panel * PANEL
        left = top // 128 * 128
        blocks = [work[p, top : top + PANEL, left:WIDE] for p in range(2)]
        panel_rows = lax.broadcasted_iota(jnp.int32, (PANEL, WIDE - left), 0)
        for k in range(min(PANEL, VALUE_ROW - top)):
            lane = top - left + k
            for p in range(2):
                block = blocks[p]
                row = block[k : k + 1, :]
                inverse = 1.0 / block[k : k + 1, lane : lane + 1]
                scaled = row * inverse
                updated = block - block[:, lane : lane + 1] * scaled
                blocks[p] = jnp.where(panel_rows == k, scaled, updated)
        for p in range(2):
            inner = top % 128
            weights = blocks[p]
            pieces = []
            if inner > 0:
                pieces.append(jnp.zeros((inner, WIDE - left), jnp.float32))
            pieces.append(weights)
            if inner + PANEL < 128:
                pieces.append(jnp.zeros((128 - inner - PANEL, WIDE - left), jnp.float32))
            tall = jnp.concatenate(pieces, axis=0) if len(pieces) > 1 else weights
            factor = work[p, :, left : left + 128]
            if panel == WIDE // PANEL - 1:
                lanes = lax.broadcasted_iota(jnp.int32, (WIDE, 128), 1)
                factor = jnp.where(lanes == VALUE_ROW - left, 0.0, factor)
            work[p, :, left:WIDE] = work[p, :, left:WIDE] - jnp.dot(
                factor, tall, precision=HIGHEST, preferred_element_type=jnp.float32
            )
            work[p, top : top + PANEL, left:WIDE] = weights

    solved = []
    for p in range(2):
        answer = jnp.where(eye, work[p, :, VALUE_ROW : VALUE_ROW + 1], 0.0)
        answer = jnp.sum(answer, axis=0, keepdims=True)
        lanes = lax.broadcasted_iota(jnp.int32, (1, WIDE), 1)
        answer = jnp.where(lanes < BLOCK, answer, 0.0)
        solved.append(answer)
        solution_ref[p : p + 1, :] = answer

    offsets = jnp.zeros((ARC_DEV, 1), jnp.float32)
    for p in range(2):
        offsets = offsets + jnp.sum(sums_ref[p] * solved[p], axis=1, keepdims=True)
    corner = lax.broadcasted_iota(jnp.int32, (ARC_DEV, 128), 0) == lax.broadcasted_iota(
        jnp.int32, (ARC_DEV, 128), 1
    )
    offset_row = jnp.sum(jnp.where(corner, offsets, 0.0), axis=0, keepdims=True)

    ranks = share_ref.shape[0]
    lines = rows_here // ranks // 128
    share_ref[...] = jnp.zeros_like(share_ref)
    for rank in range(ranks):
        share_ref[rank, lines : lines + 1, :] = offset_row

    split_rows = lax.broadcasted_iota(jnp.int32, (16, WIDE), 0)
    split = []
    for p in range(2):
        high = solved[p].astype(jnp.bfloat16).astype(jnp.float32)
        middle = (solved[p] - high).astype(jnp.bfloat16).astype(jnp.float32)
        low = solved[p] - high - middle
        stacked = jnp.where(
            split_rows == 0,
            high,
            jnp.where(split_rows == 1, middle, jnp.where(split_rows == 2, low, 0.0)),
        )
        split.append(stacked.astype(jnp.bfloat16))

    span = rows_here // ranks
    ready = 0
    for rank in range(ranks):
        while ready < parts and ready * width < (rank + 1) * span:
            copies[ready].wait()
            ready += 1
        fitted = jnp.zeros((16, span), jnp.float32)
        for p in range(2):
            fitted = fitted + jnp.dot(
                split[p],
                design[p, :, rank * span : (rank + 1) * span],
                preferred_element_type=jnp.float32,
            )
        fitted = jnp.sum(fitted, axis=0, keepdims=True)
        for line in range(lines):
            share_ref[rank, line : line + 1, :] = fitted[:, line * 128 : line * 128 + 128]


def finish_kernel(
    n,
    root_total,
    share_ref,
    arc_ref,
    value_ref,
    target_ref,
    residual_ref,
    bias_ref,
    landed,
    send,
    recv,
):
    me = lax.axis_index("ord")
    barrier = pltpu.get_barrier_semaphore()

    def greet(k, _):
        pl.semaphore_signal(
            barrier, inc=1, device_id={"ord": lax.rem(me + k, n)}, device_id_type=MESH
        )
        return 0

    lax.fori_loop(1, n, greet, 0)
    pl.semaphore_wait(barrier, n - 1)

    def scatter(k):
        peer = lax.rem(me + k, n)
        return pltpu.make_async_remote_copy(
            src_ref=share_ref.at[peer],
            dst_ref=landed.at[k],
            send_sem=send.at[k],
            recv_sem=recv.at[k],
            device_id={"ord": peer},
            device_id_type=MESH,
        )

    def start(k, _):
        scatter(k).start()
        return 0

    lax.fori_loop(1, n, start, 0)

    def add(k, summed):
        scatter(k).wait_recv()
        return summed + landed[k]

    summed = lax.fori_loop(1, n, add, share_ref[me]) / root_total
    lines = arc_ref.shape[0]
    bias = (target_ref[0:1, :] - summed[lines : lines + 1, :]) / target_ref[1:2, :]
    bias_ref[...] = bias
    arcs = arc_ref[...]
    bias_rows = jnp.zeros(arcs.shape, jnp.float32)
    for k in range(ARC_DEV):
        bias_rows = bias_rows + jnp.where(arcs == k, bias[:, k : k + 1], 0.0)
    residual_ref[...] = jnp.where(
        arcs < ARC_DEV, value_ref[...] - summed[0:lines, :] - bias_rows, 0.0
    )

    def end(k, _):
        scatter(k).wait_send()
        return 0

    lax.fori_loop(1, n, end, 0)


def per_device(obs_colat, obs_lon, obs_value, obs_arc, reg_weight):
    rows_here = obs_colat.shape[0]
    arc_devices = lax.axis_size("arc")
    order_devices = lax.axis_size("ord")
    total_rows = rows_here * arc_devices
    ord_me = lax.axis_index("ord")
    first_order = ord_me * 2 + jnp.arange(2, dtype=jnp.int32)
    grid_shape = (rows_here // 128, 128)
    steps = rows_here // CHUNK

    orders = jnp.concatenate([first_order, DEG - first_order])
    order_float = orders.astype(jnp.float32)[:, None, None]
    log_coeff = jnp.take(jnp.asarray(log_sectoral()), orders)[:, None, None]
    colat = obs_colat.reshape(grid_shape)
    lon = obs_lon.reshape(grid_shape)
    arcs = obs_arc.reshape(grid_shape)
    value = jnp.where(arcs < ARC_DEV, obs_value.reshape(grid_shape).astype(jnp.float32), 0.0)
    cosine = jnp.cos(colat)
    sectoral = jnp.exp(order_float * jnp.log(jnp.sin(colat))[None] + log_coeff)
    seeds = jnp.where(
        (arcs < ARC_DEV)[None], sectoral * jnp.cos(order_float * lon[None]), 0.0
    )
    member = jnp.arange(ARC_DEV, dtype=jnp.int32)[:, None] == obs_arc[None, :]
    counts = jnp.sum(member.astype(jnp.float32), axis=1)
    table = jnp.asarray(recursion_table(2 * order_devices).reshape(order_devices, -1))
    coef = lax.dynamic_index_in_dim(table, ord_me, keepdims=False)

    lines = CHUNK // 128
    design, normal, sums = pl.pallas_call(
        design_kernel,
        grid=(steps,),
        in_specs=[
            pl.BlockSpec(memory_space=pltpu.SMEM),
            pl.BlockSpec((lines, 128), lambda i: (i, 0)),
            pl.BlockSpec((4, lines, 128), lambda i: (0, i, 0)),
            pl.BlockSpec((lines, 128), lambda i: (i, 0)),
            pl.BlockSpec((ARC_DEV, CHUNK), lambda i: (0, i)),
            pl.BlockSpec((ARC_DEV, 128), lambda i: (0, 0)),
        ],
        out_specs=[
            pl.BlockSpec((2, ROWS, CHUNK), lambda i: (0, 0, i)),
            pl.BlockSpec((2, WIDE, WIDE), lambda i: (0, 0, 0)),
            pl.BlockSpec((2, ARC_DEV, WIDE), lambda i: (0, 0, 0)),
        ],
        out_shape=[
            jax.ShapeDtypeStruct((2, ROWS, rows_here), jnp.bfloat16),
            jax.ShapeDtypeStruct((2, WIDE, WIDE), jnp.float32),
            jax.ShapeDtypeStruct((2, ARC_DEV, WIDE), jnp.float32),
        ],
        scratch_shapes=[
            pltpu.VMEM((2 * TILES * WIDE, 128), jnp.float32),
            pltpu.VMEM((2, ROWS, WIDE), jnp.float32),
        ],
        compiler_params=pltpu.CompilerParams(vmem_limit_bytes=48 * MIB),
        name="design_normals",
    )(
        coef,
        cosine,
        seeds,
        value,
        member.astype(jnp.bfloat16),
        jnp.broadcast_to(counts[:, None], (ARC_DEV, 128)),
    )

    rows_each = 2 * WIDE // arc_devices
    summed = pl.pallas_call(
        functools.partial(reduce_kernel, arc_devices),
        in_specs=[pl.BlockSpec(memory_space=pltpu.VMEM)],
        out_specs=pl.BlockSpec(memory_space=pltpu.VMEM),
        out_shape=jax.ShapeDtypeStruct((arc_devices, rows_each, WIDE), jnp.float32),
        scratch_shapes=[pltpu.VMEM((arc_devices, rows_each, WIDE), jnp.float32)]
        + [pltpu.SemaphoreType.DMA((arc_devices,))] * 4,
        compiler_params=pltpu.CompilerParams(collective_id=0, has_side_effects=True),
        name="reduce_normals",
    )(normal.reshape(arc_devices, rows_each, WIDE))

    share_lines = rows_here // order_devices // 128
    parts = 4
    regular = jnp.concatenate(
        [reg_weight, jnp.ones((2, WIDE - BLOCK), jnp.float32)], axis=1
    ).reshape(2, 1, WIDE)
    solved, share = pl.pallas_call(
        functools.partial(solve_kernel, total_rows, parts=parts),
        in_specs=[
            pl.BlockSpec(memory_space=pltpu.VMEM),
            pl.BlockSpec(memory_space=pltpu.VMEM),
            pl.BlockSpec(memory_space=pltpu.VMEM),
            pl.BlockSpec(memory_space=pl.ANY),
        ],
        out_specs=[
            pl.BlockSpec(memory_space=pltpu.VMEM),
            pl.BlockSpec(memory_space=pltpu.VMEM),
        ],
        out_shape=[
            jax.ShapeDtypeStruct((2, WIDE), jnp.float32),
            jax.ShapeDtypeStruct((order_devices, 16, 128), jnp.float32),
        ],
        scratch_shapes=[
            pltpu.VMEM((2, WIDE, rows_here), jnp.bfloat16),
            pltpu.VMEM((2, WIDE, WIDE), jnp.float32),
            pltpu.SemaphoreType.DMA((parts,)),
        ],
        compiler_params=pltpu.CompilerParams(vmem_limit_bytes=48 * MIB),
        name="solve_fit",
    )(summed.reshape(2, WIDE, WIDE), regular, sums, design)

    local_arcs = lax.dynamic_slice_in_dim(arcs, ord_me * share_lines, share_lines)
    local_value = lax.dynamic_slice_in_dim(value, ord_me * share_lines, share_lines)
    target = jnp.stack([sums[0, :, VALUE_ROW], counts])
    target = jnp.pad(target, ((0, 6), (0, 128 - ARC_DEV)), constant_values=1.0)
    residual, bias = pl.pallas_call(
        functools.partial(finish_kernel, order_devices, math.sqrt(total_rows)),
        in_specs=[pl.BlockSpec(memory_space=pltpu.VMEM)] * 4,
        out_specs=[pl.BlockSpec(memory_space=pltpu.VMEM)] * 2,
        out_shape=[
            jax.ShapeDtypeStruct((share_lines, 128), jnp.float32),
            jax.ShapeDtypeStruct((1, 128), jnp.float32),
        ],
        scratch_shapes=[pltpu.VMEM((order_devices, 16, 128), jnp.float32)]
        + [pltpu.SemaphoreType.DMA((order_devices,))] * 2,
        compiler_params=pltpu.CompilerParams(collective_id=1, has_side_effects=True),
        name="exchange_fit",
    )(share, local_arcs, local_value, target)

    return (solved[:, :BLOCK], bias[0, :ARC_DEV], residual.reshape(-1))


def solution(mesh):
    placed = (P("arc"), P("arc"), P("arc"), P("arc"), P("ord", None))
    return jax.shard_map(
        per_device,
        mesh=mesh,
        in_specs=placed,
        out_specs=(P("ord", None), P("arc"), P(("arc", "ord"))),
        check_vma=False,
    )
```

```python
import math

import jax
import jax.numpy as jnp
import numpy as np
from jax import lax
from jax.experimental import pallas as pl
from jax.experimental.pallas import tpu as pltpu
from jax.sharding import PartitionSpec as P

DEG = 250
BLOCK = 252
ARC_DEV = 16
WIDE = 256
ROWS = WIDE + ARC_DEV
VALUE_ROW = 255
COUNT_ROW = 254
STRIDE = 20
HALF_PI = float(np.float32(0.5 * math.pi))
HALF_PI_REST = 0.5 * math.pi - HALF_PI
COSINE = [(-1.0) ** k * (2.0 * math.pi) ** (2 * k) / math.factorial(2 * k) for k in range(11)]
CHUNK = 4096
TILES = CHUNK // 128
GROUPS = CHUNK // 1024
PANEL = 64
EACH = 32
LINES = 12
MESH = pl.DeviceIdType.MESH
MIB = 1024 * 1024
HIGHEST = lax.Precision.HIGHEST


def log_sectoral():
    increments = [0.0, 0.5 * math.log(3.0)] + [
        0.5 * math.log((2.0 * degree_now + 1.0) / (2.0 * degree_now))
        for degree_now in range(2, DEG + 1)
    ]
    return np.cumsum(np.array(increments[: DEG + 1])).astype(np.float32)


def recursion_table(pairs):
    table = np.zeros((pairs, 2, WIDE), np.float64)
    table[:, 1, COUNT_ROW:] = -1.0
    for pair in range(pairs):
        for column in range(BLOCK):
            low = column < DEG + 1 - pair
            order = pair if low else DEG - pair
            degree = pair + column if low else column - 1
            if degree == order:
                table[pair, 0, column] = 0.0
                table[pair, 1, column] = -1.0
                continue
            denominator = float((degree - order) * (degree + order))
            table[pair, 0, column] = math.sqrt(
                (2.0 * degree - 1.0) * (2.0 * degree + 1.0) / denominator
            )
            table[pair, 1, column] = math.sqrt(
                max((2.0 * degree + 1.0) * (degree + order - 1.0) * (degree - order - 1.0), 0.0)
                / (denominator * max(2.0 * degree - 3.0, 1.0))
            )
    logs = log_sectoral()
    table = table.reshape(pairs // 2, 4 * WIDE)
    names = [
        [logs[q] for q in (2 * z, 2 * z + 1, DEG - 2 * z, DEG - 1 - 2 * z)]
        for z in range(pairs // 2)
    ]
    return np.concatenate([table, np.array(names), np.zeros((pairs // 2, 4))], 1).astype(
        np.float32
    )


def circle(turns, order):
    angle = turns * order
    angle = angle - jnp.floor(angle + 0.5)
    square = angle * angle
    result = jnp.full_like(square, COSINE[-1])
    for coefficient in COSINE[-2::-1]:
        result = result * square + coefficient
    return result


def polar(colat):
    x = (colat - HALF_PI) - HALF_PI_REST
    square = x * x
    odd = jnp.full_like(square, 1.0 / math.factorial(15))
    odd = -odd
    even = jnp.full_like(square, 1.0 / math.factorial(16))
    for k in range(6, -1, -1):
        odd = odd * square + (-1.0) ** k / math.factorial(2 * k + 1)
        even = even * square + (-1.0) ** (k + 1) / math.factorial(2 * k + 2)
    return -(odd * x), even * square + 1.0


def make_normals(first_pair, chunks, coef_ref, colat, lon, value, arcs, kept, design, scratch):
    window0, window1, starting, total = scratch
    starts = [DEG + 1 - first_pair, DEG - first_pair]
    chains = [(p, v) for p in range(2) for v in range(GROUPS)]
    orders = [first_pair, first_pair + 1, DEG - first_pair, DEG - 1 - first_pair]
    orders = [order.astype(jnp.float32) for order in orders]
    total[...] = jnp.zeros_like(total)
    window1[...] = jnp.zeros_like(window1)

    def chunk_body(chunk, _):
        line = pl.multiple_of(chunk * TILES, TILES)
        first_lane = pl.multiple_of(chunk * CHUNK, CHUNK)
        t = []
        for v in range(GROUPS):
            rows = pl.ds(pl.multiple_of(line + v * 8, 8), 8)
            cosine, sine = polar(colat[rows, :])
            t.append(cosine)
            log_sine = jnp.log(sine)
            turns = lon[rows, :] * (0.5 / math.pi)
            valid = arcs[rows, :] < ARC_DEV
            for q in range(4):
                sectoral = jnp.exp(orders[q] * log_sine + coef_ref[4 * WIDE + q])
                starting[q * TILES + v * 8 : q * TILES + v * 8 + 8, :] = jnp.where(
                    valid, sectoral * circle(turns, orders[q]), 0.0
                )
        kept[pl.ds(line, TILES), :] = jnp.where(
            arcs[pl.ds(line, TILES), :] < ARC_DEV,
            value[pl.ds(line, TILES), :].astype(jnp.float32),
            0.0,
        )

        def seed(q, v):
            return starting[q * TILES + v * 8 : q * TILES + v * 8 + 8, :]

        def extra(v, is_value):
            rows = pl.ds(pl.multiple_of(line + v * 8, 8), 8)
            if is_value:
                return kept[rows, :]
            return jnp.where(arcs[rows, :] < ARC_DEV, 1.0, 0.0)

        def convert(window, row):
            row = pl.multiple_of(row, 16)
            for p in range(2):
                for tile in range(TILES):
                    source = (p * TILES + tile) * STRIDE
                    lane = pl.multiple_of(first_lane + tile * 128, 128)
                    design[p, pl.ds(row, 16), pl.ds(lane, 128)] = window[
                        source : source + 16, :
                    ].astype(jnp.bfloat16)

        def columns16(window, base, carried, turning, last):
            previous, before = carried
            for inner in range(16):
                column = base + inner
                rising = [coef_ref[p * 2 * WIDE + column] for p in range(2)]
                falling = [coef_ref[p * 2 * WIDE + WIDE + column] for p in range(2)]
                current = []
                for i, (p, v) in enumerate(chains):
                    older = before[i]
                    if turning:
                        older = jnp.where(column == starts[p], seed(2 + p, v), older)
                    if last and inner >= 14:
                        older = jnp.where(
                            column == WIDE - 16 + inner, extra(v, inner == 15), older
                        )
                    now = rising[p] * (t[v] * previous[i]) - falling[p] * older
                    window[pl.ds((p * TILES + v * 8) * STRIDE + inner, 8, stride=STRIDE), :] = now
                    current.append(now)
                before, previous = previous, tuple(current)
            return previous, before

        def columns32(block, carried, turning):
            base = block * 32
            convert(window1, lax.rem(base + (WIDE - 16), WIDE))
            carried = columns16(window0, base, carried, turning, False)
            convert(window0, base)
            return columns16(window1, base + 16, carried, turning, True)

        zeros = tuple(jnp.zeros((8, 128), jnp.float32) for _ in chains)
        carried = (zeros, tuple(seed(p, v) for p, v in chains))
        turn = starts[0] // 32
        carried = lax.fori_loop(0, turn, lambda block, c: columns32(block, c, False), carried)
        carried = columns32(turn, carried, True)
        lax.fori_loop(turn + 1, WIDE // 32, lambda block, c: columns32(block, c, False), carried)
        convert(window1, WIDE - 16)

        arc_names = lax.broadcasted_iota(jnp.int32, (ARC_DEV, 128), 0)
        for tile in range(TILES):
            member = arc_names == arcs[pl.ds(line + tile, 1), :]
            member = jnp.where(member, 1.0, 0.0).astype(jnp.bfloat16)
            lane = pl.multiple_of(first_lane + tile * 128, 128)
            for p in range(2):
                design[p, WIDE:ROWS, pl.ds(lane, 128)] = member

        for p in range(2):
            total[p] += lax.dot_general(
                design[p, :, pl.ds(first_lane, CHUNK)],
                design[p, 0:WIDE, pl.ds(first_lane, CHUNK)],
                (((1,), (1,)), ((), ())),
                preferred_element_type=jnp.float32,
            )
        return 0

    lax.fori_loop(0, chunks, chunk_body, 0)


def pack_normals(total, packed):
    row_ids = lax.broadcasted_iota(jnp.int32, (128, 128), 0)
    column_ids = lax.broadcasted_iota(jnp.int32, (128, 128), 1)
    for p in range(2):
        sums = total[p, WIDE:ROWS, :]
        scaled = sums / sums[:, COUNT_ROW : COUNT_ROW + 1]
        normal = total[p, 0:WIDE, :] - lax.dot_general(
            scaled,
            sums,
            (((0,), (0,)), ((), ())),
            precision=HIGHEST,
            preferred_element_type=jnp.float32,
        )
        corner = normal[128:WIDE, 128:WIDE]
        diagonal = jnp.sum(jnp.where(row_ids == column_ids, corner, 0.0), axis=0, keepdims=True)
        packed[p * WIDE : p * WIDE + 128, :] = jnp.where(
            row_ids == BLOCK - 128, diagonal, normal[128:WIDE, 0:128]
        )
        packed[p * WIDE + 128 : p * WIDE + WIDE, :] = jnp.where(
            row_ids >= column_ids, normal[0:128, 0:128], corner
        )


def remote(axis, peer, source, target, send, recv):
    return pltpu.make_async_remote_copy(
        src_ref=source,
        dst_ref=target,
        send_sem=send,
        recv_sem=recv,
        device_id={axis: peer},
        device_id_type=MESH,
    )


def each(first, last, action):
    def body(k, _):
        action(k)
        return 0

    lax.fori_loop(first, last, body, 0)


def reduce_normals(n, packed, summed, landed, send1, recv1, send2, recv2):
    me = lax.axis_index("arc")

    def part(owner):
        return pl.ds(pl.multiple_of(owner * EACH, EACH), EACH)

    def scatter(k):
        peer = lax.rem(me + k, n)
        return remote(
            "arc", peer, packed.at[part(peer)], landed.at[k], send1.at[k], recv1.at[k]
        )

    def gather(k, owner):
        peer = lax.rem(me + k, n)
        return remote(
            "arc", peer, summed.at[part(owner)], summed.at[part(owner)], send2.at[k], recv2.at[k]
        )

    each(1, n, lambda k: scatter(k).start())

    def add(k, mine):
        scatter(k).wait_recv()
        return mine + landed[k]

    summed[part(me), :] = lax.fori_loop(1, n, add, packed[part(me), :])
    each(1, n, lambda k: gather(k, me).start())
    each(1, n, lambda k: gather(k, lax.rem(me - k + n, n)).wait_recv())

    def end():
        each(1, n, lambda k: scatter(k).wait_send())
        each(1, n, lambda k: gather(k, me).wait_send())

    return end


def build_matrix(first_pair, total_rows, summed, regular_ref, work):
    row_ids = lax.broadcasted_iota(jnp.int32, (WIDE, WIDE), 0)
    column_ids = lax.broadcasted_iota(jnp.int32, (WIDE, WIDE), 1)
    regular = jnp.concatenate(
        [regular_ref[...], jnp.ones((2, WIDE - BLOCK), jnp.float32)], axis=1
    )
    eye = row_ids == column_ids
    for p in range(2):
        left_block = summed[p * WIDE : p * WIDE + 128, :]
        mixed = summed[p * WIDE + 128 : p * WIDE + WIDE, :]
        flipped = mixed.T
        below = row_ids[0:128, 0:128] > column_ids[0:128, 0:128]
        level = eye[0:128, 0:128]
        corner = jnp.where(below, flipped, mixed)
        corner = jnp.where(level, left_block[BLOCK - 128 : BLOCK - 127, :], corner)
        upper = jnp.concatenate(
            [jnp.where(below | level, mixed, flipped), left_block.T], axis=1
        )
        normal = jnp.concatenate([upper, jnp.concatenate([left_block, corner], axis=1)], axis=0)
        border = DEG + 1 - first_pair - p
        real = (row_ids < BLOCK) & (column_ids < BLOCK)
        same = ((row_ids < border) == (column_ids < border)) & real
        matrix = jnp.where(same, normal / total_rows, 0.0)
        matrix = matrix + jnp.where(
            eye & real, regular[p : p + 1, :], jnp.where(eye, 1.0, 0.0)
        )
        right = jnp.where(row_ids < BLOCK, normal / math.sqrt(total_rows), 0.0)
        work[p] = jnp.where(column_ids == VALUE_ROW, right, matrix)


def eliminate(work):
    for panel in range(WIDE // PANEL):
        top = panel * PANEL
        left = top // 128 * 128
        blocks = [work[p, top : top + PANEL, left:WIDE] for p in range(2)]
        panel_rows = lax.broadcasted_iota(jnp.int32, (PANEL, WIDE - left), 0)
        for k in range(min(PANEL, VALUE_ROW - top)):
            lane = top - left + k
            for p in range(2):
                block = blocks[p]
                row = block[k : k + 1, :]
                inverse = 1.0 / block[k : k + 1, lane : lane + 1]
                scaled = row * inverse
                updated = block - block[:, lane : lane + 1] * scaled
                blocks[p] = jnp.where(panel_rows == k, scaled, updated)
        for p in range(2):
            inner = top % 128
            weights = blocks[p]
            pieces = []
            if inner > 0:
                pieces.append(jnp.zeros((inner, WIDE - left), jnp.float32))
            pieces.append(weights)
            if inner + PANEL < 128:
                pieces.append(jnp.zeros((128 - inner - PANEL, WIDE - left), jnp.float32))
            tall = jnp.concatenate(pieces, axis=0) if len(pieces) > 1 else weights
            factor = work[p, :, left : left + 128]
            if panel == WIDE // PANEL - 1:
                lanes = lax.broadcasted_iota(jnp.int32, (WIDE, 128), 1)
                factor = jnp.where(lanes == VALUE_ROW - left, 0.0, factor)
            work[p, :, left:WIDE] = work[p, :, left:WIDE] - jnp.dot(
                factor, tall, precision=HIGHEST, preferred_element_type=jnp.float32
            )
            work[p, top : top + PANEL, left:WIDE] = weights


def read_answer(work):
    row_ids = lax.broadcasted_iota(jnp.int32, (WIDE, WIDE), 0)
    column_ids = lax.broadcasted_iota(jnp.int32, (WIDE, WIDE), 1)
    solved = []
    for p in range(2):
        answer = jnp.where(
            row_ids == column_ids, work[p, :, VALUE_ROW : VALUE_ROW + 1], 0.0
        )
        answer = jnp.sum(answer, axis=0, keepdims=True)
        lanes = lax.broadcasted_iota(jnp.int32, (1, WIDE), 1)
        solved.append(jnp.where(lanes < BLOCK, answer, 0.0))
    return solved


def split_three(row):
    split_rows = lax.broadcasted_iota(jnp.int32, (16, WIDE), 0)
    high = row.astype(jnp.bfloat16).astype(jnp.float32)
    middle = (row - high).astype(jnp.bfloat16).astype(jnp.float32)
    low = row - high - middle
    stacked = jnp.where(
        split_rows == 0,
        high,
        jnp.where(split_rows == 1, middle, jnp.where(split_rows == 2, low, 0.0)),
    )
    return stacked.astype(jnp.bfloat16)


def whole_kernel(
    arc_devices,
    order_devices,
    rows_here,
    coef_ref,
    colat_hbm,
    lon_hbm,
    value_hbm,
    arc_hbm,
    regular_ref,
    solution_ref,
    bias_ref,
    residual_ref,
    colat,
    lon,
    value,
    arcs,
    kept,
    design,
    window0,
    window1,
    starting,
    total,
    packed,
    summed,
    landed,
    work,
    share,
    arrived,
    loaded,
    send1,
    recv1,
    send2,
    recv2,
    send3,
    recv3,
):
    total_rows = rows_here * arc_devices
    root_total = math.sqrt(total_rows)
    ord_me = lax.axis_index("ord")
    arc_me = lax.axis_index("arc")
    first_pair = ord_me * 2
    loads = []
    for i, (far, near) in enumerate(
        [(colat_hbm, colat), (lon_hbm, lon), (value_hbm, value), (arc_hbm, arcs)]
    ):
        load = pltpu.make_async_copy(far, near, loaded.at[i])
        load.start()
        loads.append(load)

    barrier = pltpu.get_barrier_semaphore()

    def greet(axis, me, n):
        each(
            1,
            n,
            lambda k: pl.semaphore_signal(
                barrier, inc=1, device_id={axis: lax.rem(me + k, n)}, device_id_type=MESH
            ),
        )

    greet("arc", arc_me, arc_devices)
    greet("ord", ord_me, order_devices)
    share[...] = jnp.zeros_like(share)
    for load in loads:
        load.wait()

    make_normals(
        first_pair,
        rows_here // CHUNK,
        coef_ref,
        colat,
        lon,
        value,
        arcs,
        kept,
        design,
        (window0, window1, starting, total),
    )
    pack_normals(total, packed)
    pl.semaphore_wait(barrier, arc_devices + order_devices - 2)
    end_reduce = reduce_normals(arc_devices, packed, summed, landed, send1, recv1, send2, recv2)
    build_matrix(first_pair, total_rows, summed, regular_ref, work)
    eliminate(work)
    solved = read_answer(work)

    square = (ARC_DEV, 128)
    corner = lax.broadcasted_iota(jnp.int32, square, 0) == lax.broadcasted_iota(
        jnp.int32, square, 1
    )
    offsets = jnp.zeros((ARC_DEV, 1), jnp.float32)
    for p in range(2):
        solution_ref[p : p + 1, :] = solved[p][:, 0:BLOCK]
        offsets = offsets + jnp.sum(total[p, WIDE:ROWS, :] * solved[p], axis=1, keepdims=True)
    offset_row = jnp.sum(jnp.where(corner, offsets, 0.0), axis=0, keepdims=True)
    split = [split_three(solved[p]) for p in range(2)]
    span = rows_here // order_devices

    def send_fit(k, source):
        peer = lax.rem(ord_me + k, order_devices)
        return remote("ord", peer, share.at[peer], arrived.at[source], send3.at[k], recv3.at[k])

    def fit(k):
        rank = lax.rem(ord_me + k, order_devices)
        lane = pl.multiple_of(rank * span, span)
        fitted = jnp.zeros((16, span), jnp.float32)
        for p in range(2):
            fitted = fitted + jnp.dot(
                split[p],
                design[p, 0:WIDE, pl.ds(lane, span)],
                preferred_element_type=jnp.float32,
            )
        fitted = jnp.sum(fitted, axis=0, keepdims=True)
        for line in range(LINES):
            share[rank, line : line + 1, :] = fitted[:, line * 128 : line * 128 + 128]
        share[rank, LINES : LINES + 1, :] = offset_row

    def fit_and_send(k):
        fit(k)
        send_fit(k, ord_me).start()

    each(1, order_devices, fit_and_send)
    fit(0)

    arrived[ord_me] = share[ord_me]
    each(
        1,
        order_devices,
        lambda k: send_fit(k, lax.rem(ord_me - k + order_devices, order_devices)).wait_recv(),
    )
    final = arrived[0]
    for source in range(1, order_devices):
        final = final + arrived[source]
    final = final / root_total
    counts = total[0, WIDE:ROWS, COUNT_ROW : COUNT_ROW + 1]
    target = total[0, WIDE:ROWS, VALUE_ROW : VALUE_ROW + 1]
    bias = jnp.where(corner, (target - final[LINES : LINES + 1, :]) / counts, 0.0)
    bias = jnp.sum(bias, axis=0, keepdims=True)
    bias_ref[...] = bias[:, 0:ARC_DEV]
    local = pl.ds(ord_me * LINES, LINES)
    my_arcs = arcs[local, :]
    bias_rows = jnp.zeros((LINES, 128), jnp.float32)
    for k in range(ARC_DEV):
        bias_rows = bias_rows + jnp.where(my_arcs == k, bias[:, k : k + 1], 0.0)
    residual_ref[...] = jnp.where(
        my_arcs < ARC_DEV, kept[local, :] - final[0:LINES, :] - bias_rows, 0.0
    )
    end_reduce()
    each(1, order_devices, lambda k: send_fit(k, ord_me).wait_send())


def per_device(obs_colat, obs_lon, obs_value, obs_arc, reg_weight):
    rows_here = obs_colat.shape[0]
    arc_devices = lax.axis_size("arc")
    order_devices = lax.axis_size("ord")
    lines = (rows_here // 128, 128)
    table = jnp.asarray(recursion_table(2 * order_devices))
    coef = lax.dynamic_index_in_dim(table, lax.axis_index("ord"), keepdims=False)

    def kernel(*refs):
        whole_kernel(arc_devices, order_devices, rows_here, *refs)

    vmem = pl.BlockSpec(memory_space=pltpu.VMEM)
    solved, bias, residual = pl.pallas_call(
        kernel,
        in_specs=[pl.BlockSpec(memory_space=pltpu.SMEM)]
        + [pl.BlockSpec(memory_space=pl.ANY)] * 4
        + [vmem],
        out_specs=[vmem] * 3,
        out_shape=[
            jax.ShapeDtypeStruct((2, BLOCK), jnp.float32),
            jax.ShapeDtypeStruct((1, ARC_DEV), jnp.float32),
            jax.ShapeDtypeStruct((LINES, 128), jnp.float32),
        ],
        scratch_shapes=[
            pltpu.VMEM(lines, jnp.float32),
            pltpu.VMEM(lines, jnp.float32),
            pltpu.VMEM(lines, jnp.bfloat16),
            pltpu.VMEM(lines, jnp.int32),
            pltpu.VMEM(lines, jnp.float32),
            pltpu.VMEM((2, ROWS, rows_here), jnp.bfloat16),
            pltpu.VMEM((2 * TILES * STRIDE, 128), jnp.float32),
            pltpu.VMEM((2 * TILES * STRIDE, 128), jnp.float32),
            pltpu.VMEM((4 * TILES, 128), jnp.float32),
            pltpu.VMEM((2, ROWS, WIDE), jnp.float32),
            pltpu.VMEM((2 * WIDE, 128), jnp.float32),
            pltpu.VMEM((2 * WIDE, 128), jnp.float32),
            pltpu.VMEM((arc_devices, EACH, 128), jnp.float32),
            pltpu.VMEM((2, WIDE, WIDE), jnp.float32),
            pltpu.VMEM((order_devices, 16, 128), jnp.float32),
            pltpu.VMEM((order_devices, 16, 128), jnp.float32),
            pltpu.SemaphoreType.DMA((4,)),
        ]
        + [pltpu.SemaphoreType.DMA((arc_devices,))] * 4
        + [pltpu.SemaphoreType.DMA((order_devices,))] * 2,
        compiler_params=pltpu.CompilerParams(
            collective_id=0, has_side_effects=True, vmem_limit_bytes=56 * MIB
        ),
        name="whole",
    )(
        coef,
        obs_colat.reshape(lines),
        obs_lon.reshape(lines),
        obs_value.reshape(lines),
        obs_arc.reshape(lines),
        reg_weight,
    )
    return (solved, bias.reshape(-1), residual.reshape(-1))


def solution(mesh):
    placed = (P("arc"), P("arc"), P("arc"), P("arc"), P("ord", None))
    return jax.shard_map(
        per_device,
        mesh=mesh,
        in_specs=placed,
        out_specs=(P("ord", None), P("arc"), P(("arc", "ord"))),
        check_vma=False,
    )
```

```python
import math

import jax
import jax.numpy as jnp
import numpy as np
from jax import lax
from jax.experimental import pallas as pl
from jax.experimental.pallas import tpu as pltpu
from jax.sharding import PartitionSpec as P

DEG = 250
BLOCK = 252
ARC_DEV = 16
WIDE = 256
ROWS = WIDE + ARC_DEV
VALUE_ROW = 255
COUNT_ROW = 254
STRIDE = 20
HALF_PI = float(np.float32(0.5 * math.pi))
HALF_PI_REST = 0.5 * math.pi - HALF_PI
COSINE = [(-1.0) ** k * (2.0 * math.pi) ** (2 * k) / math.factorial(2 * k) for k in range(11)]
CHUNK = 6144
TILES = CHUNK // 128
GROUPS = CHUNK // 1024
PANEL = 64
EACH = 32
LINES = 12
MESH = pl.DeviceIdType.MESH
MIB = 1024 * 1024
HIGHEST = lax.Precision.HIGHEST


def log_sectoral():
    increments = [0.0, 0.5 * math.log(3.0)] + [
        0.5 * math.log((2.0 * degree_now + 1.0) / (2.0 * degree_now))
        for degree_now in range(2, DEG + 1)
    ]
    return np.cumsum(np.array(increments[: DEG + 1])).astype(np.float32)


def recursion_table(pairs):
    table = np.zeros((pairs, 2, WIDE), np.float64)
    table[:, 1, COUNT_ROW:] = -1.0
    for pair in range(pairs):
        for column in range(BLOCK):
            low = column < DEG + 1 - pair
            order = pair if low else DEG - pair
            degree = pair + column if low else column - 1
            if degree == order:
                table[pair, 0, column] = 0.0
                table[pair, 1, column] = -1.0
                continue
            denominator = float((degree - order) * (degree + order))
            table[pair, 0, column] = math.sqrt(
                (2.0 * degree - 1.0) * (2.0 * degree + 1.0) / denominator
            )
            table[pair, 1, column] = math.sqrt(
                max((2.0 * degree + 1.0) * (degree + order - 1.0) * (degree - order - 1.0), 0.0)
                / (denominator * max(2.0 * degree - 3.0, 1.0))
            )
    logs = log_sectoral()
    result = np.zeros((pairs // 2, 8, WIDE), np.float32)
    result[:, 0:4] = table.reshape(pairs // 2, 4, WIDE)
    for z in range(pairs // 2):
        for q, order in enumerate((2 * z, 2 * z + 1, DEG - 2 * z, DEG - 1 - 2 * z)):
            result[z, 4, q] = logs[order]
    return result


def circle(turns, order):
    angle = turns * order
    angle = angle - jnp.floor(angle + 0.5)
    square = angle * angle
    result = jnp.full_like(square, COSINE[-1])
    for coefficient in COSINE[-2::-1]:
        result = result * square + coefficient
    return result


def polar(colat):
    x = (colat - HALF_PI) - HALF_PI_REST
    square = x * x
    odd = jnp.full_like(square, 1.0 / math.factorial(15))
    odd = -odd
    even = jnp.full_like(square, 1.0 / math.factorial(16))
    for k in range(6, -1, -1):
        odd = odd * square + (-1.0) ** k / math.factorial(2 * k + 1)
        even = even * square + (-1.0) ** (k + 1) / math.factorial(2 * k + 2)
    return -(odd * x), even * square + 1.0


def make_normals(first_pair, halves, coef_ref, colat, lon, value, arcs, kept, designs, scratch):
    window0, window1, starting, total = scratch
    starts = [DEG + 1 - first_pair, DEG - first_pair]
    chains = [(p, v) for p in range(2) for v in range(GROUPS)]
    orders = [first_pair, first_pair + 1, DEG - first_pair, DEG - 1 - first_pair]
    orders = [order.astype(jnp.float32) for order in orders]
    window1[...] = jnp.zeros_like(window1)
    kept[...] = jnp.where(arcs[...] < ARC_DEV, value[...].astype(jnp.float32), 0.0)

    def product(design, p, lane, width):
        total[p] += lax.dot_general(
            design[p, :, pl.ds(lane, width)],
            design[p, 0:WIDE, pl.ds(lane, width)],
            (((1,), (1,)), ((), ())),
            preferred_element_type=jnp.float32,
        )

    def chunk_body(half, parity):
        design, other = designs[parity], designs[1 - parity]
        line = pl.multiple_of((2 * half + parity) * TILES, TILES)
        first_lane = pl.multiple_of(half * CHUNK, CHUNK)
        other_lane = first_lane
        if parity == 0:
            other_lane = lax.rem(half + halves - 1, halves) * CHUNK
        t = []
        for v in range(GROUPS):
            rows = pl.ds(pl.multiple_of(line + v * 8, 8), 8)
            cosine, sine = polar(colat[rows, :])
            t.append(cosine)
            log_sine = jnp.log(sine)
            turns = lon[rows, :] * (0.5 / math.pi)
            valid = arcs[rows, :] < ARC_DEV
            for q in range(4):
                sectoral = jnp.exp(orders[q] * log_sine + coef_ref[4, q])
                starting[q * TILES + v * 8 : q * TILES + v * 8 + 8, :] = jnp.where(
                    valid, sectoral * circle(turns, orders[q]), 0.0
                )

        def seed(q, v):
            return starting[q * TILES + v * 8 : q * TILES + v * 8 + 8, :]

        def extra(v, is_value):
            rows = pl.ds(pl.multiple_of(line + v * 8, 8), 8)
            if is_value:
                return kept[rows, :]
            return jnp.where(arcs[rows, :] < ARC_DEV, 1.0, 0.0)

        def convert(window, row):
            row = pl.multiple_of(row, 16)
            for p in range(2):
                for tile in range(TILES):
                    source = (p * TILES + tile) * STRIDE
                    lane = pl.multiple_of(first_lane + tile * 128, 128)
                    design[p, pl.ds(row, 16), pl.ds(lane, 128)] = window[
                        source : source + 16, :
                    ].astype(jnp.bfloat16)

        def columns16(window, base, carried, turning, last):
            previous, before = carried
            for inner in range(16):
                column = base + inner
                rising = [coef_ref[2 * p, column] for p in range(2)]
                falling = [coef_ref[2 * p + 1, column] for p in range(2)]
                current = []
                for i, (p, v) in enumerate(chains):
                    older = before[i]
                    if turning:
                        older = jnp.where(column == starts[p], seed(2 + p, v), older)
                    if last and inner >= 14:
                        older = jnp.where(
                            column == WIDE - 16 + inner, extra(v, inner == 15), older
                        )
                    now = rising[p] * (t[v] * previous[i]) - falling[p] * older
                    window[pl.ds((p * TILES + v * 8) * STRIDE + inner, 8, stride=STRIDE), :] = now
                    current.append(now)
                before, previous = previous, tuple(current)
            return previous, before

        def columns32(block, carried, turning):
            base = block * 32
            quarter = CHUNK // 4
            lane = pl.multiple_of(other_lane + lax.rem(block, 4) * quarter, quarter)
            convert(window1, lax.rem(base + (WIDE - 16), WIDE))
            carried = columns16(window0, base, carried, turning, False)
            convert(window0, base)
            return columns16(window1, base + 16, carried, turning, True)

        zeros = tuple(jnp.zeros((8, 128), jnp.float32) for _ in chains)
        carried = (zeros, tuple(seed(p, v) for p, v in chains))
        turn = starts[0] // 32
        carried = lax.fori_loop(0, turn, lambda block, c: columns32(block, c, False), carried)
        carried = columns32(turn, carried, True)
        lax.fori_loop(turn + 1, WIDE // 32, lambda block, c: columns32(block, c, False), carried)
        convert(window1, WIDE - 16)

        arc_names = lax.broadcasted_iota(jnp.int32, (ARC_DEV, 128), 0)
        for tile in range(TILES):
            member = arc_names == arcs[pl.ds(line + tile, 1), :]
            member = jnp.where(member, 1.0, 0.0).astype(jnp.bfloat16)
            lane = pl.multiple_of(first_lane + tile * 128, 128)
            for p in range(2):
                design[p, WIDE:ROWS, pl.ds(lane, 128)] = member

    def two_chunks(half, _):
        for parity in range(2):
            chunk_body(half, parity)
            for p in range(2):
                product(designs[parity], p, pl.multiple_of(half * CHUNK, CHUNK), CHUNK)
        return 0

    total[...] = jnp.zeros_like(total)
    lax.fori_loop(0, halves, two_chunks, 0)


def pack_normals(total, packed):
    row_ids = lax.broadcasted_iota(jnp.int32, (128, 128), 0)
    column_ids = lax.broadcasted_iota(jnp.int32, (128, 128), 1)
    for p in range(2):
        sums = total[p, WIDE:ROWS, :]
        scaled = sums / sums[:, COUNT_ROW : COUNT_ROW + 1]
        normal = total[p, 0:WIDE, :] - lax.dot_general(
            scaled,
            sums,
            (((0,), (0,)), ((), ())),
            precision=HIGHEST,
            preferred_element_type=jnp.float32,
        )
        corner = normal[128:WIDE, 128:WIDE]
        diagonal = jnp.sum(jnp.where(row_ids == column_ids, corner, 0.0), axis=0, keepdims=True)
        packed[p * WIDE : p * WIDE + 128, :] = jnp.where(
            row_ids == BLOCK - 128, diagonal, normal[128:WIDE, 0:128]
        )
        packed[p * WIDE + 128 : p * WIDE + WIDE, :] = jnp.where(
            row_ids >= column_ids, normal[0:128, 0:128], corner
        )


def remote(axis, peer, source, target, send, recv):
    return pltpu.make_async_remote_copy(
        src_ref=source,
        dst_ref=target,
        send_sem=send,
        recv_sem=recv,
        device_id={axis: peer},
        device_id_type=MESH,
    )


def each(first, last, action):
    def body(k, _):
        action(k)
        return 0

    lax.fori_loop(first, last, body, 0)


def reduce_normals(n, packed, summed, landed, send1, recv1, send2, recv2):
    me = lax.axis_index("arc")

    def part(owner):
        return pl.ds(pl.multiple_of(owner * EACH, EACH), EACH)

    def scatter(k):
        peer = lax.rem(me + k, n)
        return remote(
            "arc", peer, packed.at[part(peer)], landed.at[k], send1.at[k], recv1.at[k]
        )

    def gather(k, owner):
        peer = lax.rem(me + k, n)
        return remote(
            "arc", peer, summed.at[part(owner)], summed.at[part(owner)], send2.at[k], recv2.at[k]
        )

    each(1, n, lambda k: scatter(k).start())

    def add(k, mine):
        scatter(k).wait_recv()
        return mine + landed[k]

    summed[part(me), :] = lax.fori_loop(1, n, add, packed[part(me), :])
    each(1, n, lambda k: gather(k, me).start())
    each(1, n, lambda k: gather(k, lax.rem(me - k + n, n)).wait_recv())

    def end():
        each(1, n, lambda k: scatter(k).wait_send())
        each(1, n, lambda k: gather(k, me).wait_send())

    return end


def build_matrix(first_pair, total_rows, summed, regular_ref, work):
    row_ids = lax.broadcasted_iota(jnp.int32, (WIDE, WIDE), 0)
    column_ids = lax.broadcasted_iota(jnp.int32, (WIDE, WIDE), 1)
    regular = jnp.concatenate(
        [regular_ref[...], jnp.ones((2, WIDE - BLOCK), jnp.float32)], axis=1
    )
    eye = row_ids == column_ids
    for p in range(2):
        left_block = summed[p * WIDE : p * WIDE + 128, :]
        mixed = summed[p * WIDE + 128 : p * WIDE + WIDE, :]
        flipped = mixed.T
        below = row_ids[0:128, 0:128] > column_ids[0:128, 0:128]
        level = eye[0:128, 0:128]
        corner = jnp.where(below, flipped, mixed)
        corner = jnp.where(level, left_block[BLOCK - 128 : BLOCK - 127, :], corner)
        upper = jnp.concatenate(
            [jnp.where(below | level, mixed, flipped), left_block.T], axis=1
        )
        normal = jnp.concatenate([upper, jnp.concatenate([left_block, corner], axis=1)], axis=0)
        border = DEG + 1 - first_pair - p
        real = (row_ids < BLOCK) & (column_ids < BLOCK)
        same = ((row_ids < border) == (column_ids < border)) & real
        matrix = jnp.where(same, normal / total_rows, 0.0)
        matrix = matrix + jnp.where(
            eye & real, regular[p : p + 1, :], jnp.where(eye, 1.0, 0.0)
        )
        right = jnp.where(row_ids < BLOCK, normal / math.sqrt(total_rows), 0.0)
        work[p] = jnp.where(column_ids == VALUE_ROW, right, matrix)


def invert_rows(rows, lane, pairs):
    names = lax.broadcasted_iota(jnp.int32, (8, 128), 0)
    spread = [jnp.broadcast_to(rows[:, lane + j : lane + j + 1], (8, 128)) for j in range(8)]
    tiles = [rows[:, i : i + 128] for i in range(0, rows.shape[1], 128)]
    for pair in range(pairs):
        top = 2 * pair
        first, second = spread[top], spread[top + 1]
        a, c = first[top : top + 1, :], first[top + 1 : top + 2, :]
        b, d = second[top : top + 1, :], second[top + 1 : top + 2, :]
        inverse = 1.0 / (a * d - b * c)
        a, b, c, d = a * inverse, b * inverse, c * inverse, d * inverse

        def step(x):
            upper, lower = x[top : top + 1, :], x[top + 1 : top + 2, :]
            new_upper = d * upper - b * lower
            new_lower = a * lower - c * upper
            x = x - first * new_upper - second * new_lower
            return jnp.where(names == top, new_upper, jnp.where(names == top + 1, new_lower, x))

        for j in range(top + 2, 2 * pairs):
            spread[j] = step(spread[j])
        tiles = [step(tile) for tile in tiles]
    return jnp.concatenate(tiles, axis=1) if len(tiles) > 1 else tiles[0]


def eliminate(work):
    for panel in range(WIDE // PANEL):
        top = panel * PANEL
        left = top // 128 * 128
        groups = [
            [work[p, top + i : top + i + 8, left:WIDE] for i in range(0, PANEL, 8)]
            for p in range(2)
        ]
        for m in range(PANEL // 8):
            lane = top - left + 8 * m
            pairs = min(4, (BLOCK - top - 8 * m) // 2)
            for p in range(2):
                solved = invert_rows(groups[p][m], lane, pairs)
                for i in range(PANEL // 8):
                    if i == m:
                        continue
                    rows = groups[p][i]
                    taken = rows[:, lane : lane + 1] * solved[0:1, :]
                    for j in range(1, 2 * pairs):
                        taken = taken + rows[:, lane + j : lane + j + 1] * solved[j : j + 1, :]
                    groups[p][i] = rows - taken
                groups[p][m] = solved
        for p in range(2):
            inner = top % 128
            weights = jnp.concatenate(groups[p], axis=0)
            pieces = []
            if inner > 0:
                pieces.append(jnp.zeros((inner, WIDE - left), jnp.float32))
            pieces.append(weights)
            if inner + PANEL < 128:
                pieces.append(jnp.zeros((128 - inner - PANEL, WIDE - left), jnp.float32))
            tall = jnp.concatenate(pieces, axis=0) if len(pieces) > 1 else weights
            factor = work[p, :, left : left + 128]
            if panel == WIDE // PANEL - 1:
                lanes = lax.broadcasted_iota(jnp.int32, (WIDE, 128), 1)
                factor = jnp.where(lanes >= BLOCK - left, 0.0, factor)
            work[p, :, left:WIDE] = work[p, :, left:WIDE] - jnp.dot(
                factor, tall, precision=HIGHEST, preferred_element_type=jnp.float32
            )
            work[p, top : top + PANEL, left:WIDE] = weights


def read_answer(work):
    row_ids = lax.broadcasted_iota(jnp.int32, (WIDE, WIDE), 0)
    column_ids = lax.broadcasted_iota(jnp.int32, (WIDE, WIDE), 1)
    solved = []
    for p in range(2):
        answer = jnp.where(
            row_ids == column_ids, work[p, :, VALUE_ROW : VALUE_ROW + 1], 0.0
        )
        answer = jnp.sum(answer, axis=0, keepdims=True)
        lanes = lax.broadcasted_iota(jnp.int32, (1, WIDE), 1)
        solved.append(jnp.where(lanes < BLOCK, answer, 0.0))
    return solved


def split_three(row):
    split_rows = lax.broadcasted_iota(jnp.int32, (16, WIDE), 0)
    high = row.astype(jnp.bfloat16).astype(jnp.float32)
    middle = (row - high).astype(jnp.bfloat16).astype(jnp.float32)
    low = row - high - middle
    stacked = jnp.where(
        split_rows == 0,
        high,
        jnp.where(split_rows == 1, middle, jnp.where(split_rows == 2, low, 0.0)),
    )
    return stacked.astype(jnp.bfloat16)


def whole_kernel(
    arc_devices,
    order_devices,
    rows_here,
    coef_hbm,
    colat_hbm,
    lon_hbm,
    value_hbm,
    arc_hbm,
    regular_ref,
    solution_ref,
    bias_ref,
    residual_ref,
    coef_ref,
    colat,
    lon,
    value,
    arcs,
    kept,
    design0,
    design1,
    window0,
    window1,
    starting,
    total,
    packed,
    summed,
    landed,
    work,
    share,
    arrived,
    loaded,
    send1,
    recv1,
    send2,
    recv2,
    send3,
    recv3,
):
    total_rows = rows_here * arc_devices
    root_total = math.sqrt(total_rows)
    ord_me = lax.axis_index("ord")
    arc_me = lax.axis_index("arc")
    first_pair = ord_me * 2
    loads = []
    for i, (far, near) in enumerate(
        [
            (coef_hbm.at[ord_me], coef_ref),
            (colat_hbm, colat),
            (lon_hbm, lon),
            (value_hbm, value),
            (arc_hbm, arcs),
        ]
    ):
        load = pltpu.make_async_copy(far, near, loaded.at[i])
        load.start()
        loads.append(load)

    barrier = pltpu.get_barrier_semaphore()

    def greet(axis, me, n):
        each(
            1,
            n,
            lambda k: pl.semaphore_signal(
                barrier, inc=1, device_id={axis: lax.rem(me + k, n)}, device_id_type=MESH
            ),
        )

    greet("arc", arc_me, arc_devices)
    greet("ord", ord_me, order_devices)
    share[...] = jnp.zeros_like(share)
    for load in loads:
        load.wait()

    make_normals(
        first_pair,
        rows_here // CHUNK // 2,
        coef_ref,
        colat,
        lon,
        value,
        arcs,
        kept,
        (design0, design1),
        (window0, window1, starting, total),
    )
    pack_normals(total, packed)
    pl.semaphore_wait(barrier, arc_devices + order_devices - 2)
    end_reduce = reduce_normals(arc_devices, packed, summed, landed, send1, recv1, send2, recv2)
    build_matrix(first_pair, total_rows, summed, regular_ref, work)
    eliminate(work)
    solved = read_answer(work)

    square = (ARC_DEV, 128)
    corner = lax.broadcasted_iota(jnp.int32, square, 0) == lax.broadcasted_iota(
        jnp.int32, square, 1
    )
    offsets = jnp.zeros((ARC_DEV, 1), jnp.float32)
    for p in range(2):
        solution_ref[p : p + 1, :] = solved[p][:, 0:BLOCK]
        offsets = offsets + jnp.sum(total[p, WIDE:ROWS, :] * solved[p], axis=1, keepdims=True)
    offset_row = jnp.sum(jnp.where(corner, offsets, 0.0), axis=0, keepdims=True)
    split = [split_three(solved[p]) for p in range(2)]
    span = rows_here // order_devices

    def send_fit(k, source):
        peer = lax.rem(ord_me + k, order_devices)
        return remote("ord", peer, share.at[peer], arrived.at[source], send3.at[k], recv3.at[k])

    def fit(design, rank, lane):
        lane = pl.multiple_of(lane, span)
        fitted = jnp.zeros((16, span), jnp.float32)
        for p in range(2):
            fitted = fitted + jnp.dot(
                split[p],
                design[p, 0:WIDE, pl.ds(lane, span)],
                preferred_element_type=jnp.float32,
            )
        fitted = jnp.sum(fitted, axis=0, keepdims=True)
        for line in range(LINES):
            share[rank, line : line + 1, :] = fitted[:, line * 128 : line * 128 + 128]
        share[rank, LINES : LINES + 1, :] = offset_row

    per_chunk = CHUNK // span
    per_half = order_devices // 2
    for parity, design in enumerate((design0, design1)):

        def fit_and_send(k, design=design, parity=parity):
            place = lax.rem(ord_me + 1 + k, per_half)
            rank = (place // per_chunk * 2 + parity) * per_chunk + lax.rem(place, per_chunk)
            fit(design, rank, place * span)

            @pl.when(rank != ord_me)
            def _():
                send_fit(lax.rem(rank - ord_me + order_devices, order_devices), ord_me).start()

        each(0, per_half, fit_and_send)

    arrived[ord_me] = share[ord_me]
    each(
        1,
        order_devices,
        lambda k: send_fit(k, lax.rem(ord_me - k + order_devices, order_devices)).wait_recv(),
    )
    final = arrived[0]
    for source in range(1, order_devices):
        final = final + arrived[source]
    final = final / root_total
    counts = total[0, WIDE:ROWS, COUNT_ROW : COUNT_ROW + 1]
    target = total[0, WIDE:ROWS, VALUE_ROW : VALUE_ROW + 1]
    bias = jnp.where(corner, (target - final[LINES : LINES + 1, :]) / counts, 0.0)
    bias = jnp.sum(bias, axis=0, keepdims=True)
    bias_ref[...] = bias[:, 0:ARC_DEV]
    local = pl.ds(ord_me * LINES, LINES)
    my_arcs = arcs[local, :]
    bias_rows = jnp.zeros((LINES, 128), jnp.float32)
    for k in range(ARC_DEV):
        bias_rows = bias_rows + jnp.where(my_arcs == k, bias[:, k : k + 1], 0.0)
    residual_ref[...] = jnp.where(
        my_arcs < ARC_DEV, kept[local, :] - final[0:LINES, :] - bias_rows, 0.0
    )
    end_reduce()
    each(1, order_devices, lambda k: send_fit(k, ord_me).wait_send())


def per_device(obs_colat, obs_lon, obs_value, obs_arc, reg_weight):
    rows_here = obs_colat.shape[0]
    arc_devices = lax.axis_size("arc")
    order_devices = lax.axis_size("ord")
    lines = (rows_here // 128, 128)
    table = jnp.asarray(recursion_table(2 * order_devices))

    def kernel(*refs):
        whole_kernel(arc_devices, order_devices, rows_here, *refs)

    vmem = pl.BlockSpec(memory_space=pltpu.VMEM)
    solved, bias, residual = pl.pallas_call(
        kernel,
        in_specs=[pl.BlockSpec(memory_space=pl.ANY)] * 5 + [vmem],
        out_specs=[vmem] * 3,
        out_shape=[
            jax.ShapeDtypeStruct((2, BLOCK), jnp.float32),
            jax.ShapeDtypeStruct((1, ARC_DEV), jnp.float32),
            jax.ShapeDtypeStruct((LINES, 128), jnp.float32),
        ],
        scratch_shapes=[
            pltpu.SMEM((8, WIDE), jnp.float32),
            pltpu.VMEM(lines, jnp.float32),
            pltpu.VMEM(lines, jnp.float32),
            pltpu.VMEM(lines, jnp.bfloat16),
            pltpu.VMEM(lines, jnp.int32),
            pltpu.VMEM(lines, jnp.float32),
            pltpu.VMEM((2, ROWS, rows_here // 2), jnp.bfloat16),
            pltpu.VMEM((2, ROWS, rows_here // 2), jnp.bfloat16),
            pltpu.VMEM((2 * TILES * STRIDE, 128), jnp.float32),
            pltpu.VMEM((2 * TILES * STRIDE, 128), jnp.float32),
            pltpu.VMEM((4 * TILES, 128), jnp.float32),
            pltpu.VMEM((2, ROWS, WIDE), jnp.float32),
            pltpu.VMEM((2 * WIDE, 128), jnp.float32),
            pltpu.VMEM((2 * WIDE, 128), jnp.float32),
            pltpu.VMEM((arc_devices, EACH, 128), jnp.float32),
            pltpu.VMEM((2, WIDE, WIDE), jnp.float32),
            pltpu.VMEM((order_devices, 16, 128), jnp.float32),
            pltpu.VMEM((order_devices, 16, 128), jnp.float32),
            pltpu.SemaphoreType.DMA((5,)),
        ]
        + [pltpu.SemaphoreType.DMA((arc_devices,))] * 4
        + [pltpu.SemaphoreType.DMA((order_devices,))] * 2,
        compiler_params=pltpu.CompilerParams(
            collective_id=0, has_side_effects=True, vmem_limit_bytes=56 * MIB
        ),
        name="whole",
    )(
        table,
        obs_colat.reshape(lines),
        obs_lon.reshape(lines),
        obs_value.reshape(lines),
        obs_arc.reshape(lines),
        reg_weight,
    )
    return (solved, bias.reshape(-1), residual.reshape(-1))


def solution(mesh):
    placed = (P("arc"), P("arc"), P("arc"), P("arc"), P("ord", None))
    return jax.shard_map(
        per_device,
        mesh=mesh,
        in_specs=placed,
        out_specs=(P("ord", None), P("arc"), P(("arc", "ord"))),
        check_vma=False,
    )
```

```python
import math

import jax
import jax.numpy as jnp
import numpy as np
from jax import lax
from jax.experimental import pallas as pl
from jax.experimental.pallas import tpu as pltpu
from jax.sharding import PartitionSpec as P

DEG = 250
BLOCK = 252
ARC_DEV = 16
WIDE = 256
ROWS = WIDE + ARC_DEV
VALUE_ROW = 255
COUNT_ROW = 254
STRIDE = 20
HALF_PI = float(np.float32(0.5 * math.pi))
HALF_PI_REST = 0.5 * math.pi - HALF_PI
COSINE = [(-1.0) ** k * (2.0 * math.pi) ** (2 * k) / math.factorial(2 * k) for k in range(11)]
CHUNK = 6144
TILES = CHUNK // 128
GROUPS = CHUNK // 1024
PANEL = 64
EACH = 32
LINES = 12
MESH = pl.DeviceIdType.MESH
MIB = 1024 * 1024
HIGHEST = lax.Precision.HIGHEST


def log_sectoral():
    increments = [0.0, 0.5 * math.log(3.0)] + [
        0.5 * math.log((2.0 * degree_now + 1.0) / (2.0 * degree_now))
        for degree_now in range(2, DEG + 1)
    ]
    return np.cumsum(np.array(increments[: DEG + 1])).astype(np.float32)


def recursion_table(pairs):
    table = np.zeros((pairs, 2, WIDE), np.float64)
    table[:, 1, COUNT_ROW:] = -1.0
    for pair in range(pairs):
        for column in range(BLOCK):
            low = column < DEG + 1 - pair
            order = pair if low else DEG - pair
            degree = pair + column if low else column - 1
            if degree == order:
                table[pair, 0, column] = 0.0
                table[pair, 1, column] = -1.0
                continue
            denominator = float((degree - order) * (degree + order))
            table[pair, 0, column] = math.sqrt(
                (2.0 * degree - 1.0) * (2.0 * degree + 1.0) / denominator
            )
            table[pair, 1, column] = math.sqrt(
                max((2.0 * degree + 1.0) * (degree + order - 1.0) * (degree - order - 1.0), 0.0)
                / (denominator * max(2.0 * degree - 3.0, 1.0))
            )
    logs = log_sectoral()
    result = np.zeros((pairs // 2, 8, WIDE), np.float32)
    result[:, 0:4] = table.reshape(pairs // 2, 4, WIDE)
    for z in range(pairs // 2):
        for q, order in enumerate((2 * z, 2 * z + 1, DEG - 2 * z, DEG - 1 - 2 * z)):
            result[z, 4, q] = logs[order]
    return result


def circle(turns, order):
    angle = turns * order
    angle = angle - jnp.floor(angle + 0.5)
    square = angle * angle
    result = jnp.full_like(square, COSINE[-1])
    for coefficient in COSINE[-2::-1]:
        result = result * square + coefficient
    return result


def polar(colat):
    x = (colat - HALF_PI) - HALF_PI_REST
    square = x * x
    odd = jnp.full_like(square, 1.0 / math.factorial(15))
    odd = -odd
    even = jnp.full_like(square, 1.0 / math.factorial(16))
    for k in range(6, -1, -1):
        odd = odd * square + (-1.0) ** k / math.factorial(2 * k + 1)
        even = even * square + (-1.0) ** (k + 1) / math.factorial(2 * k + 2)
    return -(odd * x), even * square + 1.0


def make_normals(first_pair, halves, coef_ref, colat, lon, value, arcs, kept, designs, scratch):
    window0, window1, starting, total = scratch
    starts = [DEG + 1 - first_pair, DEG - first_pair]
    chains = [(p, v) for p in range(2) for v in range(GROUPS)]
    orders = [first_pair, first_pair + 1, DEG - first_pair, DEG - 1 - first_pair]
    orders = [order.astype(jnp.float32) for order in orders]
    window1[...] = jnp.zeros_like(window1)
    kept[...] = jnp.where(arcs[...] < ARC_DEV, value[...].astype(jnp.float32), 0.0)

    def product(design, p, lane, width):
        total[p] += lax.dot_general(
            design[p, :, pl.ds(lane, width)],
            design[p, 0:WIDE, pl.ds(lane, width)],
            (((1,), (1,)), ((), ())),
            preferred_element_type=jnp.float32,
        )

    def chunk_body(half, parity):
        design, other = designs[parity], designs[1 - parity]
        line = pl.multiple_of((2 * half + parity) * TILES, TILES)
        first_lane = pl.multiple_of(half * CHUNK, CHUNK)
        other_lane = first_lane
        if parity == 0:
            other_lane = lax.rem(half + halves - 1, halves) * CHUNK
        t = []
        for v in range(GROUPS):
            rows = pl.ds(pl.multiple_of(line + v * 8, 8), 8)
            cosine, sine = polar(colat[rows, :])
            t.append(cosine)
            log_sine = jnp.log(sine)
            turns = lon[rows, :] * (0.5 / math.pi)
            valid = arcs[rows, :] < ARC_DEV
            for q in range(4):
                sectoral = jnp.exp(orders[q] * log_sine + coef_ref[4, q])
                starting[q * TILES + v * 8 : q * TILES + v * 8 + 8, :] = jnp.where(
                    valid, sectoral * circle(turns, orders[q]), 0.0
                )

        def seed(q, v):
            return starting[q * TILES + v * 8 : q * TILES + v * 8 + 8, :]

        def extra(v, is_value):
            rows = pl.ds(pl.multiple_of(line + v * 8, 8), 8)
            if is_value:
                return kept[rows, :]
            return jnp.where(arcs[rows, :] < ARC_DEV, 1.0, 0.0)

        def convert(window, row):
            row = pl.multiple_of(row, 16)
            for p in range(2):
                for tile in range(TILES):
                    source = (p * TILES + tile) * STRIDE
                    lane = pl.multiple_of(first_lane + tile * 128, 128)
                    design[p, pl.ds(row, 16), pl.ds(lane, 128)] = window[
                        source : source + 16, :
                    ].astype(jnp.bfloat16)

        def columns16(window, base, carried, turning, last):
            previous, before = carried
            for inner in range(16):
                column = base + inner
                rising = [coef_ref[2 * p, column] for p in range(2)]
                falling = [coef_ref[2 * p + 1, column] for p in range(2)]
                current = []
                for i, (p, v) in enumerate(chains):
                    older = before[i]
                    if turning:
                        older = jnp.where(column == starts[p], seed(2 + p, v), older)
                    if last and inner >= 14:
                        older = jnp.where(
                            column == WIDE - 16 + inner, extra(v, inner == 15), older
                        )
                    now = rising[p] * (t[v] * previous[i]) - falling[p] * older
                    window[pl.ds((p * TILES + v * 8) * STRIDE + inner, 8, stride=STRIDE), :] = now
                    current.append(now)
                before, previous = previous, tuple(current)
            return previous, before

        def columns32(block, carried, turning):
            base = block * 32
            quarter = CHUNK // 4
            lane = pl.multiple_of(other_lane + lax.rem(block, 4) * quarter, quarter)
            convert(window1, lax.rem(base + (WIDE - 16), WIDE))
            carried = columns16(window0, base, carried, turning, False)
            convert(window0, base)
            return columns16(window1, base + 16, carried, turning, True)

        zeros = tuple(jnp.zeros((8, 128), jnp.float32) for _ in chains)
        carried = (zeros, tuple(seed(p, v) for p, v in chains))
        turn = starts[0] // 32
        carried = lax.fori_loop(0, turn, lambda block, c: columns32(block, c, False), carried)
        carried = columns32(turn, carried, True)
        lax.fori_loop(turn + 1, WIDE // 32, lambda block, c: columns32(block, c, False), carried)
        convert(window1, WIDE - 16)

        arc_names = lax.broadcasted_iota(jnp.int32, (ARC_DEV, 128), 0)
        for tile in range(TILES):
            member = arc_names == arcs[pl.ds(line + tile, 1), :]
            member = jnp.where(member, 1.0, 0.0).astype(jnp.bfloat16)
            lane = pl.multiple_of(first_lane + tile * 128, 128)
            for p in range(2):
                design[p, WIDE:ROWS, pl.ds(lane, 128)] = member

    def two_chunks(half, _):
        for parity in range(2):
            chunk_body(half, parity)
            for p in range(2):
                product(designs[parity], p, pl.multiple_of(half * CHUNK, CHUNK), CHUNK)
        return 0

    total[...] = jnp.zeros_like(total)
    lax.fori_loop(0, halves, two_chunks, 0)


def pack_normals(total, packed):
    row_ids = lax.broadcasted_iota(jnp.int32, (128, 128), 0)
    column_ids = lax.broadcasted_iota(jnp.int32, (128, 128), 1)
    for p in range(2):
        sums = total[p, WIDE:ROWS, :]
        scaled = sums / sums[:, COUNT_ROW : COUNT_ROW + 1]
        normal = total[p, 0:WIDE, :] - lax.dot_general(
            scaled,
            sums,
            (((0,), (0,)), ((), ())),
            precision=HIGHEST,
            preferred_element_type=jnp.float32,
        )
        corner = normal[128:WIDE, 128:WIDE]
        diagonal = jnp.sum(jnp.where(row_ids == column_ids, corner, 0.0), axis=0, keepdims=True)
        packed[p * WIDE : p * WIDE + 128, :] = jnp.where(
            row_ids == BLOCK - 128, diagonal, normal[128:WIDE, 0:128]
        )
        packed[p * WIDE + 128 : p * WIDE + WIDE, :] = jnp.where(
            row_ids >= column_ids, normal[0:128, 0:128], corner
        )


def remote(axis, peer, source, target, send, recv):
    return pltpu.make_async_remote_copy(
        src_ref=source,
        dst_ref=target,
        send_sem=send,
        recv_sem=recv,
        device_id={axis: peer},
        device_id_type=MESH,
    )


def each(first, last, action):
    def body(k, _):
        action(k)
        return 0

    lax.fori_loop(first, last, body, 0)


def reduce_normals(n, packed, summed, landed, send1, recv1, send2, recv2):
    me = lax.axis_index("arc")

    def part(owner):
        return pl.ds(pl.multiple_of(owner * EACH, EACH), EACH)

    def scatter(k):
        peer = lax.rem(me + k, n)
        return remote(
            "arc", peer, packed.at[part(peer)], landed.at[k], send1.at[k], recv1.at[k]
        )

    def gather(k, owner):
        peer = lax.rem(me + k, n)
        return remote(
            "arc", peer, summed.at[part(owner)], summed.at[part(owner)], send2.at[k], recv2.at[k]
        )

    each(1, n, lambda k: scatter(k).start())

    def add(k, mine):
        scatter(k).wait_recv()
        return mine + landed[k]

    summed[part(me), :] = lax.fori_loop(1, n, add, packed[part(me), :])
    each(1, n, lambda k: gather(k, me).start())
    each(1, n, lambda k: gather(k, lax.rem(me - k + n, n)).wait_recv())

    def end():
        each(1, n, lambda k: scatter(k).wait_send())
        each(1, n, lambda k: gather(k, me).wait_send())

    return end


def build_matrix(first_pair, total_rows, summed, regular_ref, work):
    row_ids = lax.broadcasted_iota(jnp.int32, (WIDE, WIDE), 0)
    column_ids = lax.broadcasted_iota(jnp.int32, (WIDE, WIDE), 1)
    regular = jnp.concatenate(
        [regular_ref[...], jnp.ones((2, WIDE - BLOCK), jnp.float32)], axis=1
    )
    eye = row_ids == column_ids
    for p in range(2):
        left_block = summed[p * WIDE : p * WIDE + 128, :]
        mixed = summed[p * WIDE + 128 : p * WIDE + WIDE, :]
        flipped = mixed.T
        below = row_ids[0:128, 0:128] > column_ids[0:128, 0:128]
        level = eye[0:128, 0:128]
        corner = jnp.where(below, flipped, mixed)
        corner = jnp.where(level, left_block[BLOCK - 128 : BLOCK - 127, :], corner)
        upper = jnp.concatenate(
            [jnp.where(below | level, mixed, flipped), left_block.T], axis=1
        )
        normal = jnp.concatenate([upper, jnp.concatenate([left_block, corner], axis=1)], axis=0)
        border = DEG + 1 - first_pair - p
        real = (row_ids < BLOCK) & (column_ids < BLOCK)
        same = ((row_ids < border) == (column_ids < border)) & real
        matrix = jnp.where(same, normal / total_rows, 0.0)
        matrix = matrix + jnp.where(
            eye & real, regular[p : p + 1, :], jnp.where(eye, 1.0, 0.0)
        )
        right = jnp.where(row_ids < BLOCK, normal / math.sqrt(total_rows), 0.0)
        work[p] = jnp.where(column_ids == VALUE_ROW, right, matrix)


def invert_rows(rows, lane, pairs):
    names = lax.broadcasted_iota(jnp.int32, (8, 128), 0)
    spread = [jnp.broadcast_to(rows[:, lane + j : lane + j + 1], (8, 128)) for j in range(8)]
    tiles = [rows[:, i : i + 128] for i in range(0, rows.shape[1], 128)]
    for pair in range(pairs):
        top = 2 * pair
        first, second = spread[top], spread[top + 1]
        a, c = first[top : top + 1, :], first[top + 1 : top + 2, :]
        b, d = second[top : top + 1, :], second[top + 1 : top + 2, :]
        inverse = 1.0 / (a * d - b * c)
        a, b, c, d = a * inverse, b * inverse, c * inverse, d * inverse

        def step(x):
            upper, lower = x[top : top + 1, :], x[top + 1 : top + 2, :]
            new_upper = d * upper - b * lower
            new_lower = a * lower - c * upper
            x = x - first * new_upper - second * new_lower
            return jnp.where(names == top, new_upper, jnp.where(names == top + 1, new_lower, x))

        for j in range(top + 2, 2 * pairs):
            spread[j] = step(spread[j])
        tiles = [step(tile) for tile in tiles]
    return jnp.concatenate(tiles, axis=1) if len(tiles) > 1 else tiles[0]


def eliminate(work):
    for panel in range(WIDE // PANEL):
        top = panel * PANEL
        left = top // 128 * 128
        groups = [
            [work[p, top + i : top + i + 8, left:WIDE] for i in range(0, PANEL, 8)]
            for p in range(2)
        ]
        for m in range(PANEL // 8):
            lane = top - left + 8 * m
            pairs = min(4, (BLOCK - top - 8 * m) // 2)
            for p in range(2):
                solved = invert_rows(groups[p][m], lane, pairs)
                for i in range(PANEL // 8):
                    if i == m:
                        continue
                    rows = groups[p][i]
                    taken = rows[:, lane : lane + 1] * solved[0:1, :]
                    for j in range(1, 2 * pairs):
                        taken = taken + rows[:, lane + j : lane + j + 1] * solved[j : j + 1, :]
                    groups[p][i] = rows - taken
                groups[p][m] = solved
        for p in range(2):
            inner = top % 128
            weights = jnp.concatenate(groups[p], axis=0)
            pieces = []
            if inner > 0:
                pieces.append(jnp.zeros((inner, WIDE - left), jnp.float32))
            pieces.append(weights)
            if inner + PANEL < 128:
                pieces.append(jnp.zeros((128 - inner - PANEL, WIDE - left), jnp.float32))
            tall = jnp.concatenate(pieces, axis=0) if len(pieces) > 1 else weights
            factor = work[p, :, left : left + 128]
            if panel == WIDE // PANEL - 1:
                lanes = lax.broadcasted_iota(jnp.int32, (WIDE, 128), 1)
                factor = jnp.where(lanes >= BLOCK - left, 0.0, factor)
            work[p, :, left:WIDE] = work[p, :, left:WIDE] - jnp.dot(
                factor, tall, precision=HIGHEST, preferred_element_type=jnp.float32
            )
            work[p, top : top + PANEL, left:WIDE] = weights


def read_answer(work):
    row_ids = lax.broadcasted_iota(jnp.int32, (WIDE, WIDE), 0)
    column_ids = lax.broadcasted_iota(jnp.int32, (WIDE, WIDE), 1)
    solved = []
    for p in range(2):
        answer = jnp.where(
            row_ids == column_ids, work[p, :, VALUE_ROW : VALUE_ROW + 1], 0.0
        )
        answer = jnp.sum(answer, axis=0, keepdims=True)
        lanes = lax.broadcasted_iota(jnp.int32, (1, WIDE), 1)
        solved.append(jnp.where(lanes < BLOCK, answer, 0.0))
    return solved


def split_three(row):
    split_rows = lax.broadcasted_iota(jnp.int32, (16, WIDE), 0)
    high = row.astype(jnp.bfloat16).astype(jnp.float32)
    middle = (row - high).astype(jnp.bfloat16).astype(jnp.float32)
    low = row - high - middle
    stacked = jnp.where(
        split_rows == 0,
        high,
        jnp.where(split_rows == 1, middle, jnp.where(split_rows == 2, low, 0.0)),
    )
    return stacked.astype(jnp.bfloat16)


def whole_kernel(
    arc_devices,
    order_devices,
    rows_here,
    coef_hbm,
    colat_hbm,
    lon_hbm,
    value_hbm,
    arc_hbm,
    regular_ref,
    solution_ref,
    bias_ref,
    residual_ref,
    coef_ref,
    colat,
    lon,
    value,
    arcs,
    kept,
    design0,
    design1,
    window0,
    window1,
    starting,
    total,
    packed,
    summed,
    landed,
    work,
    share,
    arrived,
    loaded,
    send1,
    recv1,
    send2,
    recv2,
    send3,
    recv3,
):
    total_rows = rows_here * arc_devices
    root_total = math.sqrt(total_rows)
    ord_me = lax.axis_index("ord")
    arc_me = lax.axis_index("arc")
    first_pair = ord_me * 2
    loads = []
    for i, (far, near) in enumerate(
        [
            (coef_hbm.at[ord_me], coef_ref),
            (colat_hbm, colat),
            (lon_hbm, lon),
            (value_hbm, value),
            (arc_hbm, arcs),
        ]
    ):
        load = pltpu.make_async_copy(far, near, loaded.at[i])
        load.start()
        loads.append(load)

    barrier = pltpu.get_barrier_semaphore()

    def greet(axis, me, n):
        each(
            1,
            n,
            lambda k: pl.semaphore_signal(
                barrier, inc=1, device_id={axis: lax.rem(me + k, n)}, device_id_type=MESH
            ),
        )

    greet("arc", arc_me, arc_devices)
    greet("ord", ord_me, order_devices)
    share[...] = jnp.zeros_like(share)
    for load in loads:
        load.wait()

    make_normals(
        first_pair,
        rows_here // CHUNK // 2,
        coef_ref,
        colat,
        lon,
        value,
        arcs,
        kept,
        (design0, design1),
        (window0, window1, starting, total),
    )
    pack_normals(total, packed)
    pl.semaphore_wait(barrier, arc_devices + order_devices - 2)
    end_reduce = reduce_normals(arc_devices, packed, summed, landed, send1, recv1, send2, recv2)
    build_matrix(first_pair, total_rows, summed, regular_ref, work)
    eliminate(work)
    solved = read_answer(work)

    square = (ARC_DEV, 128)
    corner = lax.broadcasted_iota(jnp.int32, square, 0) == lax.broadcasted_iota(
        jnp.int32, square, 1
    )
    offsets = jnp.zeros((ARC_DEV, 1), jnp.float32)
    for p in range(2):
        solution_ref[p : p + 1, :] = solved[p][:, 0:BLOCK]
        offsets = offsets + jnp.sum(total[p, WIDE:ROWS, :] * solved[p], axis=1, keepdims=True)
    offset_row = jnp.sum(jnp.where(corner, offsets, 0.0), axis=0, keepdims=True)
    split = [split_three(solved[p]) for p in range(2)]
    span = rows_here // order_devices

    def send_fit(k, source):
        peer = lax.rem(ord_me + k, order_devices)
        return remote("ord", peer, share.at[peer], arrived.at[source], send3.at[k], recv3.at[k])

    def fit(design, rank, lane):
        fitted = jnp.zeros((16, span), jnp.float32)
        for p in range(2):
            fitted = fitted + jnp.dot(
                split[p],
                design[p, 0:WIDE, lane : lane + span],
                preferred_element_type=jnp.float32,
            )
        fitted = jnp.sum(fitted[0:8], axis=0, keepdims=True)
        for line in range(LINES):
            share[rank, line : line + 1, :] = fitted[:, line * 128 : line * 128 + 128]
        share[rank, LINES : LINES + 1, :] = offset_row

    per_chunk = CHUNK // span
    per_half = order_devices // 2
    for parity, design in enumerate((design0, design1)):

        def rank_of(place, parity=parity):
            return (place // per_chunk * 2 + parity) * per_chunk + lax.rem(place, per_chunk)

        for place in range(per_half):
            fit(design, (place // per_chunk * 2 + parity) * per_chunk + place % per_chunk, place * span)

        def send(k):
            rank = rank_of(lax.rem(ord_me + 1 + k, per_half))

            @pl.when(rank != ord_me)
            def _():
                send_fit(lax.rem(rank - ord_me + order_devices, order_devices), ord_me).start()

        each(0, per_half, send)

    arrived[ord_me] = share[ord_me]
    each(
        1,
        order_devices,
        lambda k: send_fit(k, lax.rem(ord_me - k + order_devices, order_devices)).wait_recv(),
    )
    final = arrived[0]
    for source in range(1, order_devices):
        final = final + arrived[source]
    final = final / root_total
    counts = total[0, WIDE:ROWS, COUNT_ROW : COUNT_ROW + 1]
    target = total[0, WIDE:ROWS, VALUE_ROW : VALUE_ROW + 1]
    bias = jnp.where(corner, (target - final[LINES : LINES + 1, :]) / counts, 0.0)
    bias = jnp.sum(bias, axis=0, keepdims=True)
    bias_ref[...] = bias[:, 0:ARC_DEV]
    local = pl.ds(ord_me * LINES, LINES)
    my_arcs = arcs[local, :]
    bias_rows = jnp.zeros((LINES, 128), jnp.float32)
    for k in range(ARC_DEV):
        bias_rows = bias_rows + jnp.where(my_arcs == k, bias[:, k : k + 1], 0.0)
    residual_ref[...] = jnp.where(
        my_arcs < ARC_DEV, kept[local, :] - final[0:LINES, :] - bias_rows, 0.0
    )
    end_reduce()
    each(1, order_devices, lambda k: send_fit(k, ord_me).wait_send())


def hand_on(*refs):
    sems = refs[6]
    copies = [pltpu.make_async_copy(refs[i], refs[3 + i], sems.at[i]) for i in range(3)]
    for copy in copies:
        copy.start()
    for copy in copies:
        copy.wait()


def per_device(obs_colat, obs_lon, obs_value, obs_arc, reg_weight):
    rows_here = obs_colat.shape[0]
    arc_devices = lax.axis_size("arc")
    order_devices = lax.axis_size("ord")
    lines = (rows_here // 128, 128)
    table = jnp.asarray(recursion_table(2 * order_devices))

    def kernel(*refs):
        whole_kernel(arc_devices, order_devices, rows_here, *refs)

    vmem = pl.BlockSpec(memory_space=pltpu.VMEM)
    solved, bias, residual = pl.pallas_call(
        kernel,
        in_specs=[pl.BlockSpec(memory_space=pl.ANY)] * 5 + [vmem],
        out_specs=[vmem] * 3,
        out_shape=[
            jax.ShapeDtypeStruct((2, BLOCK), jnp.float32),
            jax.ShapeDtypeStruct((1, ARC_DEV), jnp.float32),
            jax.ShapeDtypeStruct((LINES, 128), jnp.float32),
        ],
        scratch_shapes=[
            pltpu.SMEM((8, WIDE), jnp.float32),
            pltpu.VMEM(lines, jnp.float32),
            pltpu.VMEM(lines, jnp.float32),
            pltpu.VMEM(lines, jnp.bfloat16),
            pltpu.VMEM(lines, jnp.int32),
            pltpu.VMEM(lines, jnp.float32),
            pltpu.VMEM((2, ROWS, rows_here // 2), jnp.bfloat16),
            pltpu.VMEM((2, ROWS, rows_here // 2), jnp.bfloat16),
            pltpu.VMEM((2 * TILES * STRIDE, 128), jnp.float32),
            pltpu.VMEM((2 * TILES * STRIDE, 128), jnp.float32),
            pltpu.VMEM((4 * TILES, 128), jnp.float32),
            pltpu.VMEM((2, ROWS, WIDE), jnp.float32),
            pltpu.VMEM((2 * WIDE, 128), jnp.float32),
            pltpu.VMEM((2 * WIDE, 128), jnp.float32),
            pltpu.VMEM((arc_devices, EACH, 128), jnp.float32),
            pltpu.VMEM((2, WIDE, WIDE), jnp.float32),
            pltpu.VMEM((order_devices, 16, 128), jnp.float32),
            pltpu.VMEM((order_devices, 16, 128), jnp.float32),
            pltpu.SemaphoreType.DMA((5,)),
        ]
        + [pltpu.SemaphoreType.DMA((arc_devices,))] * 4
        + [pltpu.SemaphoreType.DMA((order_devices,))] * 2,
        compiler_params=pltpu.CompilerParams(
            collective_id=0, has_side_effects=True, vmem_limit_bytes=56 * MIB
        ),
        name="whole",
    )(
        table,
        obs_colat.reshape(lines),
        obs_lon.reshape(lines),
        obs_value.reshape(lines),
        obs_arc.reshape(lines),
        reg_weight,
    )
    shapes = [jax.ShapeDtypeStruct(x.shape, x.dtype) for x in (solved, bias, residual)]
    solved, bias, residual = pl.pallas_call(
        hand_on,
        in_specs=[pl.BlockSpec(memory_space=pl.ANY)] * 3,
        out_specs=[pl.BlockSpec(memory_space=pl.ANY)] * 3,
        out_shape=shapes,
        scratch_shapes=[pltpu.SemaphoreType.DMA((3,))],
        name="hand_on",
    )(solved, bias, residual)
    return (solved, bias.reshape(-1), residual.reshape(-1))


def solution(mesh):
    placed = (P("arc"), P("arc"), P("arc"), P("arc"), P("ord", None))
    return jax.shard_map(
        per_device,
        mesh=mesh,
        in_specs=placed,
        out_specs=(P("ord", None), P("arc"), P(("arc", "ord"))),
        check_vma=False,
    )
```

```python
import math

import jax
import jax.numpy as jnp
import numpy as np
from jax import lax
from jax.experimental import pallas as pl
from jax.experimental.pallas import tpu as pltpu
from jax.sharding import PartitionSpec as P

DEG = 250
BLOCK = 252
ARC_DEV = 16
WIDE = 256
ROWS = WIDE + ARC_DEV
VALUE_ROW = 255
COUNT_ROW = 254
STRIDE = 17
HALF_PI = float(np.float32(0.5 * math.pi))
HALF_PI_REST = 0.5 * math.pi - HALF_PI
COSINE = [(-1.0) ** k * (2.0 * math.pi) ** (2 * k) / math.factorial(2 * k) for k in range(11)]
CHUNK = 6144
TILES = CHUNK // 128
GROUPS = CHUNK // 1024
PANEL = 64
EACH = 32
LINES = 12
MESH = pl.DeviceIdType.MESH
MIB = 1024 * 1024
HIGHEST = lax.Precision.HIGHEST


def log_sectoral():
    increments = [0.0, 0.5 * math.log(3.0)] + [
        0.5 * math.log((2.0 * degree_now + 1.0) / (2.0 * degree_now))
        for degree_now in range(2, DEG + 1)
    ]
    return np.cumsum(np.array(increments[: DEG + 1])).astype(np.float32)


def recursion_table(pairs):
    table = np.zeros((pairs, 2, WIDE), np.float64)
    table[:, 1, COUNT_ROW:] = -1.0
    for pair in range(pairs):
        for column in range(BLOCK):
            low = column < DEG + 1 - pair
            order = pair if low else DEG - pair
            degree = pair + column if low else column - 1
            if degree == order:
                table[pair, 0, column] = 0.0
                table[pair, 1, column] = -1.0
                continue
            denominator = float((degree - order) * (degree + order))
            table[pair, 0, column] = math.sqrt(
                (2.0 * degree - 1.0) * (2.0 * degree + 1.0) / denominator
            )
            table[pair, 1, column] = math.sqrt(
                max((2.0 * degree + 1.0) * (degree + order - 1.0) * (degree - order - 1.0), 0.0)
                / (denominator * max(2.0 * degree - 3.0, 1.0))
            )
    logs = log_sectoral()
    result = np.zeros((pairs // 2, 8, WIDE), np.float32)
    result[:, 0:4] = table.reshape(pairs // 2, 4, WIDE)
    for z in range(pairs // 2):
        for q, order in enumerate((2 * z, 2 * z + 1, DEG - 2 * z, DEG - 1 - 2 * z)):
            result[z, 4, q] = logs[order]
    return result


def circle(turns, order):
    angle = turns * order
    angle = angle - jnp.floor(angle + 0.5)
    square = angle * angle
    result = jnp.full_like(square, COSINE[-1])
    for coefficient in COSINE[-2::-1]:
        result = result * square + coefficient
    return result


def polar(colat):
    x = (colat - HALF_PI) - HALF_PI_REST
    square = x * x
    odd = jnp.full_like(square, 1.0 / math.factorial(15))
    odd = -odd
    even = jnp.full_like(square, 1.0 / math.factorial(16))
    for k in range(6, -1, -1):
        odd = odd * square + (-1.0) ** k / math.factorial(2 * k + 1)
        even = even * square + (-1.0) ** (k + 1) / math.factorial(2 * k + 2)
    return -(odd * x), even * square + 1.0


def make_normals(first_pair, halves, coef_ref, colat, lon, value, arcs, kept, designs, scratch):
    window0, window1, starting, total = scratch
    starts = [DEG + 1 - first_pair, DEG - first_pair]
    chains = [(p, v) for p in range(2) for v in range(GROUPS)]
    orders = [first_pair, first_pair + 1, DEG - first_pair, DEG - 1 - first_pair]
    orders = [order.astype(jnp.float32) for order in orders]
    window1[...] = jnp.zeros_like(window1)
    kept[...] = jnp.where(arcs[...] < ARC_DEV, value[...].astype(jnp.float32), 0.0)

    def product(design, p, lane, width):
        total[p] += lax.dot_general(
            design[p, :, pl.ds(lane, width)],
            design[p, 0:WIDE, pl.ds(lane, width)],
            (((1,), (1,)), ((), ())),
            preferred_element_type=jnp.float32,
        )

    def chunk_body(half, parity):
        design = designs[parity]
        line = pl.multiple_of((2 * half + parity) * TILES, TILES)
        first_lane = pl.multiple_of(half * CHUNK, CHUNK)
        t = []
        for v in range(GROUPS):
            rows = pl.ds(pl.multiple_of(line + v * 8, 8), 8)
            cosine, sine = polar(colat[rows, :])
            t.append(cosine)
            log_sine = jnp.log(sine)
            turns = lon[rows, :] * (0.5 / math.pi)
            valid = arcs[rows, :] < ARC_DEV
            for q in range(4):
                sectoral = jnp.exp(orders[q] * log_sine + coef_ref[4, q])
                starting[q * TILES + v * 8 : q * TILES + v * 8 + 8, :] = jnp.where(
                    valid, sectoral * circle(turns, orders[q]), 0.0
                )

        def seed(q, v):
            return starting[q * TILES + v * 8 : q * TILES + v * 8 + 8, :]

        def extra(v, is_value):
            rows = pl.ds(pl.multiple_of(line + v * 8, 8), 8)
            if is_value:
                return kept[rows, :]
            return jnp.where(arcs[rows, :] < ARC_DEV, 1.0, 0.0)

        def convert(window, row, first=0, last=2 * TILES):
            row = pl.multiple_of(row, 16)
            for unit in range(first, last):
                p, tile = unit // TILES, unit % TILES
                lane = pl.multiple_of(first_lane + tile * 128, 128)
                design[p, pl.ds(row, 16), pl.ds(lane, 128)] = window[
                    unit * STRIDE : unit * STRIDE + 16, :
                ].astype(jnp.bfloat16)

        def columns16(window, base, carried, turning, last, done, row):
            previous, before = carried
            units = 2 * TILES // 16
            for inner in range(16):
                convert(done, row, inner * units, inner * units + units)
                column = base + inner
                rising = [coef_ref[2 * p, column] for p in range(2)]
                falling = [coef_ref[2 * p + 1, column] for p in range(2)]
                current = []
                for i, (p, v) in enumerate(chains):
                    older = before[i]
                    if turning:
                        older = jnp.where(column == starts[p], seed(2 + p, v), older)
                    if last and inner >= 14:
                        older = jnp.where(
                            column == WIDE - 16 + inner, extra(v, inner == 15), older
                        )
                    now = rising[p] * (t[v] * previous[i]) - falling[p] * older
                    window[pl.ds((p * TILES + v * 8) * STRIDE + inner, 8, stride=STRIDE), :] = now
                    current.append(now)
                before, previous = previous, tuple(current)
            return previous, before

        def columns32(block, carried, turning):
            base = block * 32
            row = lax.rem(base + (WIDE - 16), WIDE)
            carried = columns16(window0, base, carried, turning, False, window1, row)
            return columns16(window1, base + 16, carried, turning, True, window0, base)

        zeros = tuple(jnp.zeros((8, 128), jnp.float32) for _ in chains)
        carried = (zeros, tuple(seed(p, v) for p, v in chains))
        turn = starts[0] // 32
        carried = lax.fori_loop(0, turn, lambda block, c: columns32(block, c, False), carried)
        carried = columns32(turn, carried, True)
        lax.fori_loop(turn + 1, WIDE // 32, lambda block, c: columns32(block, c, False), carried)
        convert(window1, WIDE - 16)

        arc_names = lax.broadcasted_iota(jnp.int32, (ARC_DEV, 128), 0)
        for tile in range(TILES):
            member = arc_names == arcs[pl.ds(line + tile, 1), :]
            member = jnp.where(member, 1.0, 0.0).astype(jnp.bfloat16)
            lane = pl.multiple_of(first_lane + tile * 128, 128)
            for p in range(2):
                design[p, WIDE:ROWS, pl.ds(lane, 128)] = member

    def two_chunks(half, _):
        for parity in range(2):
            chunk_body(half, parity)
            for p in range(2):
                product(designs[parity], p, pl.multiple_of(half * CHUNK, CHUNK), CHUNK)
        return 0

    total[...] = jnp.zeros_like(total)
    lax.fori_loop(0, halves, two_chunks, 0)


def pack_normals(total, packed):
    row_ids = lax.broadcasted_iota(jnp.int32, (128, 128), 0)
    column_ids = lax.broadcasted_iota(jnp.int32, (128, 128), 1)
    for p in range(2):
        sums = total[p, WIDE:ROWS, :]
        scaled = sums / sums[:, COUNT_ROW : COUNT_ROW + 1]
        normal = total[p, 0:WIDE, :] - lax.dot_general(
            scaled,
            sums,
            (((0,), (0,)), ((), ())),
            precision=HIGHEST,
            preferred_element_type=jnp.float32,
        )
        corner = normal[128:WIDE, 128:WIDE]
        diagonal = jnp.sum(jnp.where(row_ids == column_ids, corner, 0.0), axis=0, keepdims=True)
        packed[p * WIDE : p * WIDE + 128, :] = jnp.where(
            row_ids == BLOCK - 128, diagonal, normal[128:WIDE, 0:128]
        )
        packed[p * WIDE + 128 : p * WIDE + WIDE, :] = jnp.where(
            row_ids >= column_ids, normal[0:128, 0:128], corner
        )


def remote(axis, peer, source, target, send, recv):
    return pltpu.make_async_remote_copy(
        src_ref=source,
        dst_ref=target,
        send_sem=send,
        recv_sem=recv,
        device_id={axis: peer},
        device_id_type=MESH,
    )


def each(first, last, action):
    def body(k, _):
        action(k)
        return 0

    lax.fori_loop(first, last, body, 0)


def reduce_normals(n, packed, summed, landed, send1, recv1, send2, recv2):
    me = lax.axis_index("arc")

    def part(owner):
        return pl.ds(pl.multiple_of(owner * EACH, EACH), EACH)

    def scatter(k):
        peer = lax.rem(me + k, n)
        return remote(
            "arc", peer, packed.at[part(peer)], landed.at[k], send1.at[k], recv1.at[k]
        )

    def gather(k, owner):
        peer = lax.rem(me + k, n)
        return remote(
            "arc", peer, summed.at[part(owner)], summed.at[part(owner)], send2.at[k], recv2.at[k]
        )

    each(1, n, lambda k: scatter(k).start())

    def add(k, mine):
        scatter(k).wait_recv()
        return mine + landed[k]

    summed[part(me), :] = lax.fori_loop(1, n, add, packed[part(me), :])
    each(1, n, lambda k: gather(k, me).start())
    each(1, n, lambda k: gather(k, lax.rem(me - k + n, n)).wait_recv())

    def end():
        each(1, n, lambda k: scatter(k).wait_send())
        each(1, n, lambda k: gather(k, me).wait_send())

    return end


def build_matrix(first_pair, total_rows, summed, regular_ref, work):
    row_ids = lax.broadcasted_iota(jnp.int32, (WIDE, WIDE), 0)
    column_ids = lax.broadcasted_iota(jnp.int32, (WIDE, WIDE), 1)
    regular = jnp.concatenate(
        [regular_ref[...], jnp.ones((2, WIDE - BLOCK), jnp.float32)], axis=1
    )
    eye = row_ids == column_ids
    for p in range(2):
        left_block = summed[p * WIDE : p * WIDE + 128, :]
        mixed = summed[p * WIDE + 128 : p * WIDE + WIDE, :]
        flipped = mixed.T
        below = row_ids[0:128, 0:128] > column_ids[0:128, 0:128]
        level = eye[0:128, 0:128]
        corner = jnp.where(below, flipped, mixed)
        corner = jnp.where(level, left_block[BLOCK - 128 : BLOCK - 127, :], corner)
        upper = jnp.concatenate(
            [jnp.where(below | level, mixed, flipped), left_block.T], axis=1
        )
        normal = jnp.concatenate([upper, jnp.concatenate([left_block, corner], axis=1)], axis=0)
        border = DEG + 1 - first_pair - p
        real = (row_ids < BLOCK) & (column_ids < BLOCK)
        same = ((row_ids < border) == (column_ids < border)) & real
        matrix = jnp.where(same, normal / total_rows, 0.0)
        matrix = matrix + jnp.where(
            eye & real, regular[p : p + 1, :], jnp.where(eye, 1.0, 0.0)
        )
        right = jnp.where(row_ids < BLOCK, normal / math.sqrt(total_rows), 0.0)
        work[p] = jnp.where(column_ids == VALUE_ROW, right, matrix)


def invert_rows(rows, lane, pairs):
    names = lax.broadcasted_iota(jnp.int32, (8, 128), 0)
    spread = [jnp.broadcast_to(rows[:, lane + j : lane + j + 1], (8, 128)) for j in range(8)]
    tiles = [rows[:, i : i + 128] for i in range(0, rows.shape[1], 128)]
    for pair in range(pairs):
        top = 2 * pair
        first, second = spread[top], spread[top + 1]
        a, c = first[top : top + 1, :], first[top + 1 : top + 2, :]
        b, d = second[top : top + 1, :], second[top + 1 : top + 2, :]
        inverse = 1.0 / (a * d - b * c)
        a, b, c, d = a * inverse, b * inverse, c * inverse, d * inverse

        def step(x):
            upper, lower = x[top : top + 1, :], x[top + 1 : top + 2, :]
            new_upper = d * upper - b * lower
            new_lower = a * lower - c * upper
            x = x - first * new_upper - second * new_lower
            return jnp.where(names == top, new_upper, jnp.where(names == top + 1, new_lower, x))

        for j in range(top + 2, 2 * pairs):
            spread[j] = step(spread[j])
        tiles = [step(tile) for tile in tiles]
    return jnp.concatenate(tiles, axis=1) if len(tiles) > 1 else tiles[0]


def eliminate(work):
    for panel in range(WIDE // PANEL):
        top = panel * PANEL
        left = top // 128 * 128
        groups = [
            [work[p, top + i : top + i + 8, left:WIDE] for i in range(0, PANEL, 8)]
            for p in range(2)
        ]
        for m in range(PANEL // 8):
            lane = top - left + 8 * m
            pairs = min(4, (BLOCK - top - 8 * m) // 2)
            for p in range(2):
                solved = invert_rows(groups[p][m], lane, pairs)
                for i in range(PANEL // 8):
                    if i == m:
                        continue
                    rows = groups[p][i]
                    taken = rows[:, lane : lane + 1] * solved[0:1, :]
                    for j in range(1, 2 * pairs):
                        taken = taken + rows[:, lane + j : lane + j + 1] * solved[j : j + 1, :]
                    groups[p][i] = rows - taken
                groups[p][m] = solved
        for p in range(2):
            inner = top % 128
            weights = jnp.concatenate(groups[p], axis=0)
            pieces = []
            if inner > 0:
                pieces.append(jnp.zeros((inner, WIDE - left), jnp.float32))
            pieces.append(weights)
            if inner + PANEL < 128:
                pieces.append(jnp.zeros((128 - inner - PANEL, WIDE - left), jnp.float32))
            tall = jnp.concatenate(pieces, axis=0) if len(pieces) > 1 else weights
            factor = work[p, :, left : left + 128]
            if panel == WIDE // PANEL - 1:
                lanes = lax.broadcasted_iota(jnp.int32, (WIDE, 128), 1)
                factor = jnp.where(lanes >= BLOCK - left, 0.0, factor)
            work[p, :, left:WIDE] = work[p, :, left:WIDE] - jnp.dot(
                factor, tall, precision=HIGHEST, preferred_element_type=jnp.float32
            )
            work[p, top : top + PANEL, left:WIDE] = weights


def read_answer(work):
    row_ids = lax.broadcasted_iota(jnp.int32, (WIDE, WIDE), 0)
    column_ids = lax.broadcasted_iota(jnp.int32, (WIDE, WIDE), 1)
    solved = []
    for p in range(2):
        answer = jnp.where(
            row_ids == column_ids, work[p, :, VALUE_ROW : VALUE_ROW + 1], 0.0
        )
        answer = jnp.sum(answer, axis=0, keepdims=True)
        lanes = lax.broadcasted_iota(jnp.int32, (1, WIDE), 1)
        solved.append(jnp.where(lanes < BLOCK, answer, 0.0))
    return solved


def split_three(row):
    split_rows = lax.broadcasted_iota(jnp.int32, (16, WIDE), 0)
    high = row.astype(jnp.bfloat16).astype(jnp.float32)
    middle = (row - high).astype(jnp.bfloat16).astype(jnp.float32)
    low = row - high - middle
    stacked = jnp.where(
        split_rows == 0,
        high,
        jnp.where(split_rows == 1, middle, jnp.where(split_rows == 2, low, 0.0)),
    )
    return stacked.astype(jnp.bfloat16)


def whole_kernel(
    arc_devices,
    order_devices,
    rows_here,
    coef_hbm,
    colat_hbm,
    lon_hbm,
    value_hbm,
    arc_hbm,
    regular_ref,
    solution_ref,
    bias_ref,
    residual_ref,
    coef_ref,
    colat,
    lon,
    value,
    arcs,
    kept,
    design0,
    design1,
    window0,
    window1,
    starting,
    total,
    packed,
    summed,
    landed,
    work,
    share,
    arrived,
    loaded,
    send1,
    recv1,
    send2,
    recv2,
    send3,
    recv3,
):
    total_rows = rows_here * arc_devices
    root_total = math.sqrt(total_rows)
    ord_me = lax.axis_index("ord")
    arc_me = lax.axis_index("arc")
    first_pair = ord_me * 2
    loads = []
    for i, (far, near) in enumerate(
        [
            (coef_hbm.at[ord_me], coef_ref),
            (colat_hbm, colat),
            (lon_hbm, lon),
            (value_hbm, value),
            (arc_hbm, arcs),
        ]
    ):
        load = pltpu.make_async_copy(far, near, loaded.at[i])
        load.start()
        loads.append(load)

    barrier = pltpu.get_barrier_semaphore()

    def greet(axis, me, n):
        each(
            1,
            n,
            lambda k: pl.semaphore_signal(
                barrier, inc=1, device_id={axis: lax.rem(me + k, n)}, device_id_type=MESH
            ),
        )

    greet("arc", arc_me, arc_devices)
    greet("ord", ord_me, order_devices)
    share[...] = jnp.zeros_like(share)
    for load in loads:
        load.wait()

    make_normals(
        first_pair,
        rows_here // CHUNK // 2,
        coef_ref,
        colat,
        lon,
        value,
        arcs,
        kept,
        (design0, design1),
        (window0, window1, starting, total),
    )
    pack_normals(total, packed)
    pl.semaphore_wait(barrier, arc_devices + order_devices - 2)
    end_reduce = reduce_normals(arc_devices, packed, summed, landed, send1, recv1, send2, recv2)
    build_matrix(first_pair, total_rows, summed, regular_ref, work)
    eliminate(work)
    solved = read_answer(work)

    square = (ARC_DEV, 128)
    corner = lax.broadcasted_iota(jnp.int32, square, 0) == lax.broadcasted_iota(
        jnp.int32, square, 1
    )
    offsets = jnp.zeros((ARC_DEV, 1), jnp.float32)
    for p in range(2):
        solution_ref[p : p + 1, :] = solved[p][:, 0:BLOCK]
        offsets = offsets + jnp.sum(total[p, WIDE:ROWS, :] * solved[p], axis=1, keepdims=True)
    offset_row = jnp.sum(jnp.where(corner, offsets, 0.0), axis=0, keepdims=True)
    split = [split_three(solved[p]) for p in range(2)]
    span = rows_here // order_devices

    def send_fit(k, source):
        peer = lax.rem(ord_me + k, order_devices)
        return remote("ord", peer, share.at[peer], arrived.at[source], send3.at[k], recv3.at[k])

    def fit(design, rank, lane):
        fitted = jnp.zeros((16, span), jnp.float32)
        for p in range(2):
            fitted = fitted + jnp.dot(
                split[p],
                design[p, 0:WIDE, lane : lane + span],
                preferred_element_type=jnp.float32,
            )
        fitted = jnp.sum(fitted[0:8], axis=0, keepdims=True)
        for line in range(LINES):
            share[rank, line : line + 1, :] = fitted[:, line * 128 : line * 128 + 128]
        share[rank, LINES : LINES + 1, :] = offset_row

    per_chunk = CHUNK // span
    per_half = order_devices // 2
    for parity, design in enumerate((design0, design1)):

        def rank_of(place, parity=parity):
            return (place // per_chunk * 2 + parity) * per_chunk + lax.rem(place, per_chunk)

        for place in range(per_half):
            fit(design, (place // per_chunk * 2 + parity) * per_chunk + place % per_chunk, place * span)

        def send(k):
            rank = rank_of(lax.rem(ord_me + 1 + k, per_half))

            @pl.when(rank != ord_me)
            def _():
                send_fit(lax.rem(rank - ord_me + order_devices, order_devices), ord_me).start()

        each(0, per_half, send)

    arrived[ord_me] = share[ord_me]
    each(
        1,
        order_devices,
        lambda k: send_fit(k, lax.rem(ord_me - k + order_devices, order_devices)).wait_recv(),
    )
    final = arrived[0]
    for source in range(1, order_devices):
        final = final + arrived[source]
    final = final / root_total
    counts = total[0, WIDE:ROWS, COUNT_ROW : COUNT_ROW + 1]
    target = total[0, WIDE:ROWS, VALUE_ROW : VALUE_ROW + 1]
    bias = jnp.where(corner, (target - final[LINES : LINES + 1, :]) / counts, 0.0)
    bias = jnp.sum(bias, axis=0, keepdims=True)
    bias_ref[...] = bias[:, 0:ARC_DEV]
    local = pl.ds(ord_me * LINES, LINES)
    my_arcs = arcs[local, :]
    bias_rows = jnp.zeros((LINES, 128), jnp.float32)
    for k in range(ARC_DEV):
        bias_rows = bias_rows + jnp.where(my_arcs == k, bias[:, k : k + 1], 0.0)
    residual_ref[...] = jnp.where(
        my_arcs < ARC_DEV, kept[local, :] - final[0:LINES, :] - bias_rows, 0.0
    )
    end_reduce()
    each(1, order_devices, lambda k: send_fit(k, ord_me).wait_send())


def hand_on(*refs):
    sems = refs[6]
    copies = [pltpu.make_async_copy(refs[i], refs[3 + i], sems.at[i]) for i in range(3)]
    for copy in copies:
        copy.start()
    for copy in copies:
        copy.wait()


def per_device(obs_colat, obs_lon, obs_value, obs_arc, reg_weight):
    rows_here = obs_colat.shape[0]
    arc_devices = lax.axis_size("arc")
    order_devices = lax.axis_size("ord")
    lines = (rows_here // 128, 128)
    table = jnp.asarray(recursion_table(2 * order_devices))

    def kernel(*refs):
        whole_kernel(arc_devices, order_devices, rows_here, *refs)

    vmem = pl.BlockSpec(memory_space=pltpu.VMEM)
    solved, bias, residual = pl.pallas_call(
        kernel,
        in_specs=[pl.BlockSpec(memory_space=pl.ANY)] * 5 + [vmem],
        out_specs=[vmem] * 3,
        out_shape=[
            jax.ShapeDtypeStruct((2, BLOCK), jnp.float32),
            jax.ShapeDtypeStruct((1, ARC_DEV), jnp.float32),
            jax.ShapeDtypeStruct((LINES, 128), jnp.float32),
        ],
        scratch_shapes=[
            pltpu.SMEM((8, WIDE), jnp.float32),
            pltpu.VMEM(lines, jnp.float32),
            pltpu.VMEM(lines, jnp.float32),
            pltpu.VMEM(lines, jnp.bfloat16),
            pltpu.VMEM(lines, jnp.int32),
            pltpu.VMEM(lines, jnp.float32),
            pltpu.VMEM((2, ROWS, rows_here // 2), jnp.bfloat16),
            pltpu.VMEM((2, ROWS, rows_here // 2), jnp.bfloat16),
            pltpu.VMEM((2 * TILES * STRIDE, 128), jnp.float32),
            pltpu.VMEM((2 * TILES * STRIDE, 128), jnp.float32),
            pltpu.VMEM((4 * TILES, 128), jnp.float32),
            pltpu.VMEM((2, ROWS, WIDE), jnp.float32),
            pltpu.VMEM((2 * WIDE, 128), jnp.float32),
            pltpu.VMEM((2 * WIDE, 128), jnp.float32),
            pltpu.VMEM((arc_devices, EACH, 128), jnp.float32),
            pltpu.VMEM((2, WIDE, WIDE), jnp.float32),
            pltpu.VMEM((order_devices, 16, 128), jnp.float32),
            pltpu.VMEM((order_devices, 16, 128), jnp.float32),
            pltpu.SemaphoreType.DMA((5,)),
        ]
        + [pltpu.SemaphoreType.DMA((arc_devices,))] * 4
        + [pltpu.SemaphoreType.DMA((order_devices,))] * 2,
        compiler_params=pltpu.CompilerParams(
            collective_id=0, has_side_effects=True, vmem_limit_bytes=56 * MIB
        ),
        name="whole",
    )(
        table,
        obs_colat.reshape(lines),
        obs_lon.reshape(lines),
        obs_value.reshape(lines),
        obs_arc.reshape(lines),
        reg_weight,
    )
    shapes = [jax.ShapeDtypeStruct(x.shape, x.dtype) for x in (solved, bias, residual)]
    solved, bias, residual = pl.pallas_call(
        hand_on,
        in_specs=[pl.BlockSpec(memory_space=pl.ANY)] * 3,
        out_specs=[pl.BlockSpec(memory_space=pl.ANY)] * 3,
        out_shape=shapes,
        scratch_shapes=[pltpu.SemaphoreType.DMA((3,))],
        name="hand_on",
    )(solved, bias, residual)
    return (solved, bias.reshape(-1), residual.reshape(-1))


def solution(mesh):
    placed = (P("arc"), P("arc"), P("arc"), P("arc"), P("ord", None))
    return jax.shard_map(
        per_device,
        mesh=mesh,
        in_specs=placed,
        out_specs=(P("ord", None), P("arc"), P(("arc", "ord"))),
        check_vma=False,
    )
```

```python
import math

import jax
import jax.numpy as jnp
import numpy as np
from jax import lax
from jax.experimental import pallas as pl
from jax.experimental.pallas import tpu as pltpu
from jax.sharding import PartitionSpec as P

DEG = 250
BLOCK = 252
ARC_DEV = 16
WIDE = 256
ROWS = WIDE + ARC_DEV
VALUE_ROW = 255
COUNT_ROW = 254
STRIDE = 17
HALF_PI = float(np.float32(0.5 * math.pi))
HALF_PI_REST = 0.5 * math.pi - HALF_PI
COSINE = [(-1.0) ** k * (2.0 * math.pi) ** (2 * k) / math.factorial(2 * k) for k in range(11)]
CHUNK = 6144
TILES = CHUNK // 128
GROUPS = CHUNK // 1024
PANEL = 64
EACH = 32
LINES = 12
MESH = pl.DeviceIdType.MESH
MIB = 1024 * 1024
HIGHEST = lax.Precision.HIGHEST


def log_sectoral():
    increments = [0.0, 0.5 * math.log(3.0)] + [
        0.5 * math.log((2.0 * degree_now + 1.0) / (2.0 * degree_now))
        for degree_now in range(2, DEG + 1)
    ]
    return np.cumsum(np.array(increments[: DEG + 1])).astype(np.float32)


def recursion_table(pairs):
    table = np.zeros((pairs, 2, WIDE), np.float64)
    table[:, 1, COUNT_ROW:] = -1.0
    for pair in range(pairs):
        for column in range(BLOCK):
            low = column < DEG + 1 - pair
            order = pair if low else DEG - pair
            degree = pair + column if low else column - 1
            if degree == order:
                table[pair, 0, column] = 0.0
                table[pair, 1, column] = -1.0
                continue
            denominator = float((degree - order) * (degree + order))
            table[pair, 0, column] = math.sqrt(
                (2.0 * degree - 1.0) * (2.0 * degree + 1.0) / denominator
            )
            table[pair, 1, column] = math.sqrt(
                max((2.0 * degree + 1.0) * (degree + order - 1.0) * (degree - order - 1.0), 0.0)
                / (denominator * max(2.0 * degree - 3.0, 1.0))
            )
    logs = log_sectoral()
    result = np.zeros((pairs // 2, 8, WIDE), np.float32)
    result[:, 0:4] = table.reshape(pairs // 2, 4, WIDE)
    for z in range(pairs // 2):
        for q, order in enumerate((2 * z, 2 * z + 1, DEG - 2 * z, DEG - 1 - 2 * z)):
            result[z, 4, q] = logs[order]
    return result


def circle(turns, order):
    angle = turns * order
    angle = angle - jnp.floor(angle + 0.5)
    square = angle * angle
    result = jnp.full_like(square, COSINE[-1])
    for coefficient in COSINE[-2::-1]:
        result = result * square + coefficient
    return result


def polar(colat):
    x = (colat - HALF_PI) - HALF_PI_REST
    square = x * x
    odd = jnp.full_like(square, 1.0 / math.factorial(15))
    odd = -odd
    even = jnp.full_like(square, 1.0 / math.factorial(16))
    for k in range(6, -1, -1):
        odd = odd * square + (-1.0) ** k / math.factorial(2 * k + 1)
        even = even * square + (-1.0) ** (k + 1) / math.factorial(2 * k + 2)
    return -(odd * x), even * square + 1.0


def make_normals(first_pair, halves, coef_ref, colat, lon, value, arcs, kept, designs, scratch):
    window0, window1, starting, total = scratch
    starts = [DEG + 1 - first_pair, DEG - first_pair]
    chains = [(p, v) for p in range(2) for v in range(GROUPS)]
    orders = [first_pair, first_pair + 1, DEG - first_pair, DEG - 1 - first_pair]
    orders = [order.astype(jnp.float32) for order in orders]
    window1[...] = jnp.zeros_like(window1)
    kept[...] = jnp.where(arcs[...] < ARC_DEV, value[...].astype(jnp.float32), 0.0)

    def product(design, p, lane, width):
        total[p] += lax.dot_general(
            design[p, :, pl.ds(lane, width)],
            design[p, 0:WIDE, pl.ds(lane, width)],
            (((1,), (1,)), ((), ())),
            preferred_element_type=jnp.float32,
        )

    def chunk_body(half, parity):
        design = designs[parity]
        line = pl.multiple_of((2 * half + parity) * TILES, TILES)
        first_lane = pl.multiple_of(half * CHUNK, CHUNK)
        t = []
        for v in range(GROUPS):
            rows = pl.ds(pl.multiple_of(line + v * 8, 8), 8)
            cosine, sine = polar(colat[rows, :])
            t.append(cosine)
            log_sine = jnp.log(sine)
            turns = lon[rows, :] * (0.5 / math.pi)
            valid = arcs[rows, :] < ARC_DEV
            for q in range(4):
                sectoral = jnp.exp(orders[q] * log_sine + coef_ref[4, q])
                starting[q * TILES + v * 8 : q * TILES + v * 8 + 8, :] = jnp.where(
                    valid, sectoral * circle(turns, orders[q]), 0.0
                )

        def seed(q, v):
            return starting[q * TILES + v * 8 : q * TILES + v * 8 + 8, :]

        def extra(v, is_value):
            rows = pl.ds(pl.multiple_of(line + v * 8, 8), 8)
            if is_value:
                return kept[rows, :]
            return jnp.where(arcs[rows, :] < ARC_DEV, 1.0, 0.0)

        def convert(window, row, first=0, last=2 * TILES):
            row = pl.multiple_of(row, 16)
            for unit in range(first, last):
                p, tile = unit // TILES, unit % TILES
                lane = pl.multiple_of(first_lane + tile * 128, 128)
                design[p, pl.ds(row, 16), pl.ds(lane, 128)] = window[
                    unit * STRIDE : unit * STRIDE + 16, :
                ].astype(jnp.bfloat16)

        def columns16(window, base, carried, turning, last, done, row):
            previous, before = carried
            units = 2 * TILES // 16
            for inner in range(16):
                convert(done, row, inner * units, inner * units + units)
                column = base + inner
                rising = [coef_ref[2 * p, column] for p in range(2)]
                falling = [coef_ref[2 * p + 1, column] for p in range(2)]
                current = []
                for i, (p, v) in enumerate(chains):
                    older = before[i]
                    if turning:
                        older = jnp.where(column == starts[p], seed(2 + p, v), older)
                    if last and inner >= 14:
                        older = jnp.where(
                            column == WIDE - 16 + inner, extra(v, inner == 15), older
                        )
                    now = rising[p] * (t[v] * previous[i]) - falling[p] * older
                    window[pl.ds((p * TILES + v * 8) * STRIDE + inner, 8, stride=STRIDE), :] = now
                    current.append(now)
                before, previous = previous, tuple(current)
            return previous, before

        def columns32(block, carried, turning):
            base = block * 32
            row = lax.rem(base + (WIDE - 16), WIDE)
            carried = columns16(window0, base, carried, turning, False, window1, row)
            return columns16(window1, base + 16, carried, turning, True, window0, base)

        zeros = tuple(jnp.zeros((8, 128), jnp.float32) for _ in chains)
        carried = (zeros, tuple(seed(p, v) for p, v in chains))
        turn = starts[0] // 32
        carried = lax.fori_loop(0, turn, lambda block, c: columns32(block, c, False), carried)
        carried = columns32(turn, carried, True)
        lax.fori_loop(turn + 1, WIDE // 32, lambda block, c: columns32(block, c, False), carried)
        convert(window1, WIDE - 16)

        arc_names = lax.broadcasted_iota(jnp.int32, (ARC_DEV, 128), 0)
        for tile in range(TILES):
            member = arc_names == arcs[pl.ds(line + tile, 1), :]
            member = jnp.where(member, 1.0, 0.0).astype(jnp.bfloat16)
            lane = pl.multiple_of(first_lane + tile * 128, 128)
            for p in range(2):
                design[p, WIDE:ROWS, pl.ds(lane, 128)] = member

    def two_chunks(half, _):
        for parity in range(2):
            chunk_body(half, parity)
            for p in range(2):
                product(designs[parity], p, pl.multiple_of(half * CHUNK, CHUNK), CHUNK)
        return 0

    total[...] = jnp.zeros_like(total)
    lax.fori_loop(0, halves, two_chunks, 0)


def pack_normals(total, packed):
    row_ids = lax.broadcasted_iota(jnp.int32, (128, 128), 0)
    column_ids = lax.broadcasted_iota(jnp.int32, (128, 128), 1)
    for p in range(2):
        sums = total[p, WIDE:ROWS, :]
        scaled = sums / sums[:, COUNT_ROW : COUNT_ROW + 1]
        normal = total[p, 0:WIDE, :] - lax.dot_general(
            scaled,
            sums,
            (((0,), (0,)), ((), ())),
            precision=HIGHEST,
            preferred_element_type=jnp.float32,
        )
        corner = normal[128:WIDE, 128:WIDE]
        diagonal = jnp.sum(jnp.where(row_ids == column_ids, corner, 0.0), axis=0, keepdims=True)
        packed[p * WIDE : p * WIDE + 128, :] = jnp.where(
            row_ids == BLOCK - 128, diagonal, normal[128:WIDE, 0:128]
        )
        packed[p * WIDE + 128 : p * WIDE + WIDE, :] = jnp.where(
            row_ids >= column_ids, normal[0:128, 0:128], corner
        )


def remote(axis, peer, source, target, send, recv):
    return pltpu.make_async_remote_copy(
        src_ref=source,
        dst_ref=target,
        send_sem=send,
        recv_sem=recv,
        device_id={axis: peer},
        device_id_type=MESH,
    )


def each(first, last, action):
    def body(k, _):
        action(k)
        return 0

    lax.fori_loop(first, last, body, 0)


def reduce_normals(n, packed, summed, landed, send1, recv1, send2, recv2):
    me = lax.axis_index("arc")

    def part(owner):
        return pl.ds(pl.multiple_of(owner * EACH, EACH), EACH)

    def scatter(k):
        peer = lax.rem(me + k, n)
        return remote(
            "arc", peer, packed.at[part(peer)], landed.at[k], send1.at[k], recv1.at[k]
        )

    def gather(k, owner):
        peer = lax.rem(me + k, n)
        return remote(
            "arc", peer, summed.at[part(owner)], summed.at[part(owner)], send2.at[k], recv2.at[k]
        )

    each(1, n, lambda k: scatter(k).start())

    def add(k, mine):
        scatter(k).wait_recv()
        return mine + landed[k]

    summed[part(me), :] = lax.fori_loop(1, n, add, packed[part(me), :])
    each(1, n, lambda k: gather(k, me).start())
    each(1, n, lambda k: gather(k, lax.rem(me - k + n, n)).wait_recv())

    def end():
        each(1, n, lambda k: scatter(k).wait_send())
        each(1, n, lambda k: gather(k, me).wait_send())

    return end


def build_matrix(first_pair, total_rows, summed, regular_ref, work):
    row_ids = lax.broadcasted_iota(jnp.int32, (WIDE, WIDE), 0)
    column_ids = lax.broadcasted_iota(jnp.int32, (WIDE, WIDE), 1)
    regular = jnp.concatenate(
        [regular_ref[...], jnp.ones((2, WIDE - BLOCK), jnp.float32)], axis=1
    )
    eye = row_ids == column_ids
    for p in range(2):
        left_block = summed[p * WIDE : p * WIDE + 128, :]
        mixed = summed[p * WIDE + 128 : p * WIDE + WIDE, :]
        flipped = mixed.T
        below = row_ids[0:128, 0:128] > column_ids[0:128, 0:128]
        level = eye[0:128, 0:128]
        corner = jnp.where(below, flipped, mixed)
        corner = jnp.where(level, left_block[BLOCK - 128 : BLOCK - 127, :], corner)
        upper = jnp.concatenate(
            [jnp.where(below | level, mixed, flipped), left_block.T], axis=1
        )
        normal = jnp.concatenate([upper, jnp.concatenate([left_block, corner], axis=1)], axis=0)
        border = DEG + 1 - first_pair - p
        real = (row_ids < BLOCK) & (column_ids < BLOCK)
        same = ((row_ids < border) == (column_ids < border)) & real
        matrix = jnp.where(same, normal / total_rows, 0.0)
        matrix = matrix + jnp.where(
            eye & real, regular[p : p + 1, :], jnp.where(eye, 1.0, 0.0)
        )
        right = jnp.where(row_ids < BLOCK, normal / math.sqrt(total_rows), 0.0)
        work[p] = jnp.where(column_ids == VALUE_ROW, right, matrix)


def invert_rows(rows, lane, pairs):
    names = lax.broadcasted_iota(jnp.int32, (8, 128), 0)
    spread = [jnp.broadcast_to(rows[:, lane + j : lane + j + 1], (8, 128)) for j in range(8)]
    tiles = [rows[:, i : i + 128] for i in range(0, rows.shape[1], 128)]
    for pair in range(pairs):
        top = 2 * pair
        first, second = spread[top], spread[top + 1]
        a, c = first[top : top + 1, :], first[top + 1 : top + 2, :]
        b, d = second[top : top + 1, :], second[top + 1 : top + 2, :]
        inverse = 1.0 / (a * d - b * c)
        a, b, c, d = a * inverse, b * inverse, c * inverse, d * inverse

        def step(x):
            upper, lower = x[top : top + 1, :], x[top + 1 : top + 2, :]
            new_upper = d * upper - b * lower
            new_lower = a * lower - c * upper
            x = x - first * new_upper - second * new_lower
            return jnp.where(names == top, new_upper, jnp.where(names == top + 1, new_lower, x))

        for j in range(top + 2, 2 * pairs):
            spread[j] = step(spread[j])
        tiles = [step(tile) for tile in tiles]
    return jnp.concatenate(tiles, axis=1) if len(tiles) > 1 else tiles[0]


def eliminate(work):
    for panel in range(WIDE // PANEL):
        top = panel * PANEL
        left = top // 128 * 128
        groups = [
            [work[p, top + i : top + i + 8, left:WIDE] for i in range(0, PANEL, 8)]
            for p in range(2)
        ]
        for m in range(PANEL // 8):
            lane = top - left + 8 * m
            pairs = min(4, (BLOCK - top - 8 * m) // 2)
            for p in range(2):
                solved = invert_rows(groups[p][m], lane, pairs)
                for i in range(PANEL // 8):
                    if i == m:
                        continue
                    rows = groups[p][i]
                    taken = rows[:, lane : lane + 1] * solved[0:1, :]
                    for j in range(1, 2 * pairs):
                        taken = taken + rows[:, lane + j : lane + j + 1] * solved[j : j + 1, :]
                    groups[p][i] = rows - taken
                groups[p][m] = solved
        for p in range(2):
            inner = top % 128
            weights = jnp.concatenate(groups[p], axis=0)
            pieces = []
            if inner > 0:
                pieces.append(jnp.zeros((inner, WIDE - left), jnp.float32))
            pieces.append(weights)
            if inner + PANEL < 128:
                pieces.append(jnp.zeros((128 - inner - PANEL, WIDE - left), jnp.float32))
            tall = jnp.concatenate(pieces, axis=0) if len(pieces) > 1 else weights
            factor = work[p, :, left : left + 128]
            if panel == WIDE // PANEL - 1:
                lanes = lax.broadcasted_iota(jnp.int32, (WIDE, 128), 1)
                factor = jnp.where(lanes >= BLOCK - left, 0.0, factor)
            work[p, :, left:WIDE] = work[p, :, left:WIDE] - jnp.dot(
                factor, tall, precision=HIGHEST, preferred_element_type=jnp.float32
            )
            work[p, top : top + PANEL, left:WIDE] = weights


def read_answer(work):
    row_ids = lax.broadcasted_iota(jnp.int32, (WIDE, WIDE), 0)
    column_ids = lax.broadcasted_iota(jnp.int32, (WIDE, WIDE), 1)
    solved = []
    for p in range(2):
        answer = jnp.where(
            row_ids == column_ids, work[p, :, VALUE_ROW : VALUE_ROW + 1], 0.0
        )
        answer = jnp.sum(answer, axis=0, keepdims=True)
        lanes = lax.broadcasted_iota(jnp.int32, (1, WIDE), 1)
        solved.append(jnp.where(lanes < BLOCK, answer, 0.0))
    return solved


def split_three(row):
    split_rows = lax.broadcasted_iota(jnp.int32, (16, WIDE), 0)
    high = row.astype(jnp.bfloat16).astype(jnp.float32)
    middle = (row - high).astype(jnp.bfloat16).astype(jnp.float32)
    low = row - high - middle
    stacked = jnp.where(
        split_rows == 0,
        high,
        jnp.where(split_rows == 1, middle, jnp.where(split_rows == 2, low, 0.0)),
    )
    return stacked.astype(jnp.bfloat16)


def whole_kernel(
    arc_devices,
    order_devices,
    rows_here,
    coef_hbm,
    colat_hbm,
    lon_hbm,
    value_hbm,
    arc_hbm,
    regular_ref,
    solution_ref,
    bias_ref,
    residual_ref,
    coef_ref,
    colat,
    lon,
    value,
    arcs,
    kept,
    design0,
    design1,
    window0,
    window1,
    starting,
    total,
    packed,
    summed,
    landed,
    work,
    share,
    arrived,
    loaded,
    send1,
    recv1,
    send2,
    recv2,
    send3,
    recv3,
):
    total_rows = rows_here * arc_devices
    root_total = math.sqrt(total_rows)
    ord_me = lax.axis_index("ord")
    arc_me = lax.axis_index("arc")
    first_pair = ord_me * 2
    loads = []
    for i, (far, near) in enumerate(
        [
            (coef_hbm.at[ord_me], coef_ref),
            (colat_hbm, colat),
            (lon_hbm, lon),
            (value_hbm, value),
            (arc_hbm, arcs),
        ]
    ):
        load = pltpu.make_async_copy(far, near, loaded.at[i])
        load.start()
        loads.append(load)

    barrier = pltpu.get_barrier_semaphore()

    def greet(axis, me, n):
        each(
            1,
            n,
            lambda k: pl.semaphore_signal(
                barrier, inc=1, device_id={axis: lax.rem(me + k, n)}, device_id_type=MESH
            ),
        )

    greet("arc", arc_me, arc_devices)
    greet("ord", ord_me, order_devices)
    share[...] = jnp.zeros_like(share)
    for load in loads:
        load.wait()

    make_normals(
        first_pair,
        rows_here // CHUNK // 2,
        coef_ref,
        colat,
        lon,
        value,
        arcs,
        kept,
        (design0, design1),
        (window0, window1, starting, total),
    )
    pack_normals(total, packed)
    pl.semaphore_wait(barrier, arc_devices + order_devices - 2)
    end_reduce = reduce_normals(arc_devices, packed, summed, landed, send1, recv1, send2, recv2)
    build_matrix(first_pair, total_rows, summed, regular_ref, work)
    eliminate(work)
    solved = read_answer(work)

    square = (ARC_DEV, 128)
    corner = lax.broadcasted_iota(jnp.int32, square, 0) == lax.broadcasted_iota(
        jnp.int32, square, 1
    )
    offsets = jnp.zeros((ARC_DEV, 1), jnp.float32)
    for p in range(2):
        solution_ref[p : p + 1, :] = solved[p][:, 0:BLOCK]
        offsets = offsets + jnp.sum(total[p, WIDE:ROWS, :] * solved[p], axis=1, keepdims=True)
    offset_row = jnp.sum(jnp.where(corner, offsets, 0.0), axis=0, keepdims=True)
    split = [split_three(solved[p]) for p in range(2)]
    span = rows_here // order_devices

    def send_fit(k, source):
        peer = lax.rem(ord_me + k, order_devices)
        return remote("ord", peer, share.at[peer], arrived.at[source], send3.at[k], recv3.at[k])

    def fit(design, rank, lane):
        fitted = jnp.zeros((16, span), jnp.float32)
        for p in range(2):
            fitted = fitted + jnp.dot(
                split[p],
                design[p, 0:WIDE, lane : lane + span],
                preferred_element_type=jnp.float32,
            )
        fitted = jnp.sum(fitted[0:8], axis=0, keepdims=True)
        for line in range(LINES):
            share[rank, line : line + 1, :] = fitted[:, line * 128 : line * 128 + 128]
        share[rank, LINES : LINES + 1, :] = offset_row

    per_chunk = CHUNK // span
    per_half = order_devices // 2
    for parity, design in enumerate((design0, design1)):

        def rank_of(place, parity=parity):
            return (place // per_chunk * 2 + parity) * per_chunk + lax.rem(place, per_chunk)

        for first in range(0, per_half, per_chunk):
            for place in range(first, first + per_chunk):
                owner = (first // per_chunk * 2 + parity) * per_chunk + place - first
                fit(design, owner, place * span)

            def send(k, first=first, rank_of=rank_of):
                rank = rank_of(first + lax.rem(ord_me + 1 + k, per_chunk))

                @pl.when(rank != ord_me)
                def _():
                    send_fit(
                        lax.rem(rank - ord_me + order_devices, order_devices), ord_me
                    ).start()

            each(0, per_chunk, send)

    arrived[ord_me] = share[ord_me]
    each(
        1,
        order_devices,
        lambda k: send_fit(k, lax.rem(ord_me - k + order_devices, order_devices)).wait_recv(),
    )
    final = arrived[0]
    for source in range(1, order_devices):
        final = final + arrived[source]
    final = final / root_total
    counts = total[0, WIDE:ROWS, COUNT_ROW : COUNT_ROW + 1]
    target = total[0, WIDE:ROWS, VALUE_ROW : VALUE_ROW + 1]
    bias = jnp.where(corner, (target - final[LINES : LINES + 1, :]) / counts, 0.0)
    bias = jnp.sum(bias, axis=0, keepdims=True)
    bias_ref[...] = bias[:, 0:ARC_DEV]
    local = pl.ds(ord_me * LINES, LINES)
    my_arcs = arcs[local, :]
    bias_rows = jnp.zeros((LINES, 128), jnp.float32)
    for k in range(ARC_DEV):
        bias_rows = bias_rows + jnp.where(my_arcs == k, bias[:, k : k + 1], 0.0)
    residual_ref[...] = jnp.where(
        my_arcs < ARC_DEV, kept[local, :] - final[0:LINES, :] - bias_rows, 0.0
    )
    end_reduce()
    each(1, order_devices, lambda k: send_fit(k, ord_me).wait_send())


def hand_on(*refs):
    sems = refs[6]
    copies = [pltpu.make_async_copy(refs[i], refs[3 + i], sems.at[i]) for i in range(3)]
    for copy in copies:
        copy.start()
    for copy in copies:
        copy.wait()


def per_device(obs_colat, obs_lon, obs_value, obs_arc, reg_weight):
    rows_here = obs_colat.shape[0]
    arc_devices = lax.axis_size("arc")
    order_devices = lax.axis_size("ord")
    lines = (rows_here // 128, 128)
    table = jnp.asarray(recursion_table(2 * order_devices))

    def kernel(*refs):
        whole_kernel(arc_devices, order_devices, rows_here, *refs)

    vmem = pl.BlockSpec(memory_space=pltpu.VMEM)
    solved, bias, residual = pl.pallas_call(
        kernel,
        in_specs=[pl.BlockSpec(memory_space=pl.ANY)] * 5 + [vmem],
        out_specs=[vmem] * 3,
        out_shape=[
            jax.ShapeDtypeStruct((2, BLOCK), jnp.float32),
            jax.ShapeDtypeStruct((1, ARC_DEV), jnp.float32),
            jax.ShapeDtypeStruct((LINES, 128), jnp.float32),
        ],
        scratch_shapes=[
            pltpu.SMEM((8, WIDE), jnp.float32),
            pltpu.VMEM(lines, jnp.float32),
            pltpu.VMEM(lines, jnp.float32),
            pltpu.VMEM(lines, jnp.bfloat16),
            pltpu.VMEM(lines, jnp.int32),
            pltpu.VMEM(lines, jnp.float32),
            pltpu.VMEM((2, ROWS, rows_here // 2), jnp.bfloat16),
            pltpu.VMEM((2, ROWS, rows_here // 2), jnp.bfloat16),
            pltpu.VMEM((2 * TILES * STRIDE, 128), jnp.float32),
            pltpu.VMEM((2 * TILES * STRIDE, 128), jnp.float32),
            pltpu.VMEM((4 * TILES, 128), jnp.float32),
            pltpu.VMEM((2, ROWS, WIDE), jnp.float32),
            pltpu.VMEM((2 * WIDE, 128), jnp.float32),
            pltpu.VMEM((2 * WIDE, 128), jnp.float32),
            pltpu.VMEM((arc_devices, EACH, 128), jnp.float32),
            pltpu.VMEM((2, WIDE, WIDE), jnp.float32),
            pltpu.VMEM((order_devices, 16, 128), jnp.float32),
            pltpu.VMEM((order_devices, 16, 128), jnp.float32),
            pltpu.SemaphoreType.DMA((5,)),
        ]
        + [pltpu.SemaphoreType.DMA((arc_devices,))] * 4
        + [pltpu.SemaphoreType.DMA((order_devices,))] * 2,
        compiler_params=pltpu.CompilerParams(
            collective_id=0, has_side_effects=True, vmem_limit_bytes=56 * MIB
        ),
        name="whole",
    )(
        table,
        obs_colat.reshape(lines),
        obs_lon.reshape(lines),
        obs_value.reshape(lines),
        obs_arc.reshape(lines),
        reg_weight,
    )
    shapes = [jax.ShapeDtypeStruct(x.shape, x.dtype) for x in (solved, bias, residual)]
    solved, bias, residual = pl.pallas_call(
        hand_on,
        in_specs=[pl.BlockSpec(memory_space=pl.ANY)] * 3,
        out_specs=[pl.BlockSpec(memory_space=pl.ANY)] * 3,
        out_shape=shapes,
        scratch_shapes=[pltpu.SemaphoreType.DMA((3,))],
        name="hand_on",
    )(solved, bias, residual)
    return (solved, bias.reshape(-1), residual.reshape(-1))


def solution(mesh):
    placed = (P("arc"), P("arc"), P("arc"), P("arc"), P("ord", None))
    return jax.shard_map(
        per_device,
        mesh=mesh,
        in_specs=placed,
        out_specs=(P("ord", None), P("arc"), P(("arc", "ord"))),
        check_vma=False,
    )
```
